256 devices in a mesh: aux: 16 (over x_hi, z), row: 16 (over y, x_lo, core).
Axes of the slice: x: 4 (x_hi: 2, x_lo: 2; x = x_hi * 2 + x_lo), y: 4, z: 8, core: 2. Of those that a mesh axis runs over, the one named last changes fastest.
Arguments:
- factors: float32 [48, 3072, 3072], P('aux', 'row'), may hold values from -0.109375 to 0.109375
- orbitals: float32 [3072, 512], P('row'), may hold values from -1.25 to 1.25
- tile_mask: int32 [48, 24, 24], P('aux'), may hold values from 0 to 1, as said below
Outputs:
- exchange: float32 [3072, 3072], P('aux', 'row')
The draws below stay inside these ranges and needn't reach their ends.
Inputs may be any that keep to these rules, and one draw needn't show every extreme that they name: `tile_mask`: each auxiliary function has its own share of surviving tiles, from about three tenths to all of them.
All inputs are finite; a program needn't handle non-finite values.
Results may differ from the reference program's by a relative error of at most 0.0001.
Values sent between devices are 32-bit elements; how exact they have to be, the bound alone decides.
A program may use at most 128 MiB of HBM per device.

```python
import jax
import jax.numpy as jnp
from jax import lax

NBF = 3072
NOCC = 512
TILE = 128
NT = 24
NAUX = 48


def draw_tile_mask(key, part):
    key = jax.random.fold_in(key, 5)
    first, second = jax.random.split(key)
    level = jax.random.randint(first, (NAUX, 1, 1), 3, 11)
    values = jax.random.randint(second, (NAUX, NT, NT), 0, 10)
    return (values < level).astype(jnp.int32)


def shard_levels(rng, extent, pieces, low, high):
    def one(axis_at, shards_of):
        heights = jax.random.uniform(jax.random.fold_in(jax.random.fold_in(rng, 6), axis_at), (shards_of,), jnp.float32, low / len(pieces), high / len(pieces))
        return jnp.repeat(jnp.exp(heights), extent[axis_at] // shards_of).reshape((-1,) + (1,) * (len(extent) - axis_at - 1))

    factor_of = one(*pieces[0])
    for cut in pieces[1:]:
        factor_of = factor_of * one(*cut)
    return factor_of


def gaussian(key, dims, spread, limit, pieces=(), held_as=jnp.bfloat16):
    loudness = shard_levels(key, dims, pieces, -0.22, 0.18) if pieces else 1.0
    drawn = jax.random.normal(key, dims, jnp.float32) * spread * loudness
    return jnp.minimum(jnp.maximum(drawn, -limit), limit).astype(held_as)


def setup_inputs(seed: int = 0) -> dict:
    keys = jax.random.split(jax.random.key(seed), 4)
    return {
        "factors": gaussian(keys[0], (NAUX, NBF, NBF), NBF ** -0.5, 0.109375, ((0, 16), (1, 16)), jnp.float32),
        "orbitals": gaussian(keys[1], (NBF, NOCC), 0.08, 1.25, ((0, 16),), jnp.float32),
        "tile_mask": draw_tile_mask(jax.random.fold_in(keys[3], 71), 0),
    }


def reference(factors, orbitals, tile_mask):
    def accumulate(total, pair):
        slab, mask = pair
        full = jnp.repeat(jnp.repeat(mask.astype(jnp.float32), TILE, axis=0), TILE, axis=1)
        half = jnp.dot(slab * full, orbitals, precision=lax.Precision.HIGHEST, preferred_element_type=jnp.float32)
        total = total + jnp.dot(half, half.T, precision=lax.Precision.HIGHEST, preferred_element_type=jnp.float32)
        return total, None

    start = jnp.zeros((NBF, NBF), jnp.float32)
    total, unused = lax.scan(accumulate, start, (factors, tile_mask))
    return total
```

```python
import jax
import jax.numpy as jnp
from jax import lax
from jax.experimental import pallas as pl
from jax.experimental.pallas import tpu as pltpu
from jax.sharding import PartitionSpec as P

F32 = jnp.float32
BF16 = jnp.bfloat16
MESH = pl.DeviceIdType.MESH
ROWS = 192
PAIR = 384
LANES = 128
CHUNKS = 4
SLABS = 3
STRIP = 24
STEPS_Y = (1, -1, 2)


def split(value):
    high = value.astype(BF16)
    return high, (value - high.astype(F32)).astype(BF16)


def kernel(
    b_hbm, c_ref, mask, out,
    bf, bh, bl, cb, ch, hs, ho, hy, hx, hw, left, right, kp, rc, rp, rm, fp, rd, rt,
    sem_b, y_send, y_recv, x_send, x_recv, s_send, s_recv,
    h_send, ho_recv, hy_recv, hx_recv, hw_recv,
    core_send, core_recv, p_send, p_recv, m_send, m_recv, f_send, f_recv,
):
    a, r = lax.axis_index("aux"), lax.axis_index("row")
    xh, z = a // 8, a % 8
    y, xl, c = r // 4, (r // 2) % 2, r % 2
    sib = 1 - c

    def row_of(yy, xx, cc):
        return ((yy + 4) % 4 * 2 + xx) * 2 + cc

    def dev(yy, xx, cc):
        return (a, row_of(yy, xx, cc))

    def copy(src, dst, send, recv, to):
        return pltpu.make_async_remote_copy(
            src_ref=src, dst_ref=dst, send_sem=send, recv_sem=recv, device_id=to, device_id_type=MESH
        )

    across = ((a, row_of(y, 1 - xl, c)), ((1 - xh) * 8 + z, row_of(y, 1 - xl, c)))
    sibling = dev(y, xl, sib)
    z_up = (xh * 8 + (z + 1) % 8, r)
    z_down = (xh * 8 + (z + 7) % 8, r)

    slab_copies = [pltpu.make_async_copy(b_hbm.at[p], bf.at[p], sem_b.at[p]) for p in range(SLABS)]
    for each in slab_copies:
        each.start()

    barrier = pltpu.get_barrier_semaphore()
    greeted = [
        dev(y + 1, xl, c), dev(y - 1, xl, c), dev(y + 2, xl, c), across[0], across[1], sibling,
        dev(y + 1, xl, sib), dev(y, 1 - xl, sib), dev(y + 2, xl, sib), z_up, z_down,
    ]
    for each in greeted:
        pl.semaphore_signal(barrier, inc=1, device_id=each, device_id_type=MESH)
    for k in range(CHUNKS):
        cb[k, r] = c_ref[:, k * LANES : (k + 1) * LANES]
    pl.semaphore_wait(barrier, len(greeted))

    def to_y(k, j):
        return copy(cb.at[k, r], cb.at[k, r], y_send.at[k, j], y_recv.at[k, j], dev(y + STEPS_Y[j], xl, c))

    def from_y(k, j):
        block = row_of(y - STEPS_Y[j], xl, c)
        return copy(cb.at[k, block], cb.at[k, block], y_send.at[k, j], y_recv.at[k, j], sibling)

    def to_x(k, j, block, part):
        piece = cb.at[k, block, pl.ds(96 * part, 96)]
        return copy(piece, piece, x_send.at[k, j, part], x_recv.at[k, j, part], across[part])

    def to_sibling(k, j, block):
        return copy(cb.at[k, block], cb.at[k, block], s_send.at[k, j], s_recv.at[k, j], sibling)

    def y_block(j, xx, cc):
        return row_of(y - STEPS_Y[j], xx, cc) if j < 3 else row_of(y, xx, cc)

    def first(k):
        for j in range(3):
            to_y(k, j).start()
        for part in range(2):
            to_x(k, 3, r, part).start()
        to_sibling(k, 3, r).start()

    def forward_y(k):
        for j in range(3):
            from_y(k, j).wait_recv()
            block = y_block(j, xl, c)
            for part in range(2):
                to_x(k, j, block, part).start()
            to_sibling(k, j, block).start()

    def forward_x(k):
        for j in (3, 0, 1, 2):
            block = y_block(j, 1 - xl, c)
            for part in range(2):
                to_x(k, j, block, part).wait_recv()
            to_sibling(k, 4 + j, block).start()

    def whole(k):
        for j in range(4):
            to_sibling(k, j, y_block(j, xl, sib)).wait_recv()
            to_sibling(k, 4 + j, y_block(j, 1 - xl, sib)).wait_recv()

    def screen(p):
        slab_copies[p].wait()

        def tile(n, _):
            at = pl.ds(pl.multiple_of(n * LANES, LANES), LANES)
            for g in range(3):
                keep = mask[p, (3 * r + g) // 2, n].astype(F32)
                rows = pl.ds(64 * g, 64)
                high, low = split(bf[p, rows, at] * keep)
                bh[p, rows, at] = high
                bl[p, rows, at] = low
            return 0

        lax.fori_loop(0, 24, tile, 0, unroll=4)

    def half(k):
        def block(n, _):
            high, low = split(cb[k, n])
            at = pl.ds(pl.multiple_of(n * ROWS, ROWS), ROWS)
            ch[at, 0:LANES] = high
            ch[at, LANES : 2 * LANES] = low
            return 0

        lax.fori_loop(0, 16, block, 0)

        def slab(p, _):
            both = jnp.dot(bh[p], ch[...], preferred_element_type=F32)
            low = jnp.dot(bl[p], ch[:, 0:LANES], preferred_element_type=F32)
            hs[k, p] = both[:, 0:LANES] + (both[:, LANES : 2 * LANES] + low)
            return 0

        lax.fori_loop(0, SLABS, slab, 0)

    def h_copies(k):
        h, q = k % 2, k // 2
        return (
            copy(hs.at[k], hy.at[q, c], h_send.at[k, 0], hy_recv.at[q, c], dev(y - 1, xl, h)),
            copy(hs.at[k], hx.at[q, c], h_send.at[k, 1], hx_recv.at[q, c], dev(y, 1 - xl, h)),
            copy(hs.at[k], hw.at[c], h_send.at[k, 2], hw_recv.at[c], dev(y + 2, xl, h)),
            copy(hs.at[k], ho.at[q], h_send.at[k, 3], ho_recv.at[q], sibling),
        )

    def send_half(k):
        to_1, to_2, to_3, to_4 = h_copies(k)
        to_1.start()
        to_2.start()
        pl.when(k // 2 == 1 - y // 2)(to_3.start)
        pl.when(k % 2 != c)(to_4.start)

    first(0)
    first(1)
    kp[...] = jnp.zeros_like(kp)
    screen(0)
    forward_y(0)
    first(2)
    screen(1)
    forward_y(1)
    first(3)
    forward_x(0)
    screen(2)

    def step(k, _):
        @pl.when(k < CHUNKS - 2)
        def _():
            forward_y(k + 2)

        @pl.when(k < CHUNKS - 1)
        def _():
            forward_x(k + 1)

        whole(k)
        half(k)
        send_half(k)
        return 0

    lax.fori_loop(0, CHUNKS, step, 0)

    def operand(slot, core, p, value):
        rows = pl.ds(pl.multiple_of(core * ROWS, ROWS), ROWS)
        high, low = split(value)
        for where, part in ((0, high), (1, low), (2, high)):
            left[slot, rows, pl.ds((where * SLABS + p) * LANES, LANES)] = part
        if slot in (0, 2):
            for where, part in ((0, high), (1, high), (2, low)):
                right[slot // 2, rows, pl.ds((where * SLABS + p) * LANES, LANES)] = part

    def product(kind, _):
        g, t = kind // 3, kind % 3
        value = lax.dot_general(
            left[2 * g + (t + 1) // 2], right[t // 2], (((1,), (1,)), ((), ())), preferred_element_type=F32
        )
        kp[kind] = kp[kind] + value.reshape(8, 2, STRIP, PAIR)
        return 0

    def core_copy(g):
        kinds = pl.ds(3 * g, 3)
        return copy(kp.at[kinds, :, sib], rc.at[kinds], core_send.at[g], core_recv.at[g], sibling)

    def core_arrival(g):
        kinds = pl.ds(3 * g, 3)
        return copy(rc.at[kinds], rc.at[kinds], core_send.at[g], core_recv.at[g], sibling)

    def products(q, _):
        k = 2 * q + c
        copy(ho.at[q], ho.at[q], h_send.at[k, 3], ho_recv.at[q], sibling).wait_recv()
        for core in range(2):
            copy(hy.at[q, core], hy.at[q, core], h_send.at[k, 0], hy_recv.at[q, core], sibling).wait_recv()
            copy(hx.at[q, core], hx.at[q, core], h_send.at[k, 1], hx_recv.at[q, core], sibling).wait_recv()
        for p in range(SLABS):
            operand(0, c, p, hs[k, p])
            operand(0, sib, p, ho[q, p])
            for core in range(2):
                operand(1, core, p, hy[q, core, p])
                operand(2, core, p, hx[q, core, p])
        lax.fori_loop(0, 3, product, 0)

        @pl.when(q == 1)
        def _():
            core_copy(0).start()

        @pl.when(q == xl)
        def _():
            lax.fori_loop(3, 4, product, 0)

        @pl.when(q == y // 2)
        def _():
            for core in range(2):
                copy(hw.at[core], hw.at[core], h_send.at[k, 2], hw_recv.at[core], sibling).wait_recv()
            for p in range(SLABS):
                for core in range(2):
                    operand(3, core, p, hw[core, p])
            lax.fori_loop(4, 6, product, 0)

        return 0

    lax.fori_loop(0, 2, products, 0)
    core_copy(1).start()

    def up_copy(s, g):
        kinds = pl.ds(3 * g, 3)
        return copy(rc.at[kinds, (z + 4 - s) % 8], rp.at[s, kinds], p_send.at[s, g], p_recv.at[s, g], z_up)

    def down_copy(s, g):
        kinds = pl.ds(3 * g, 3)
        return copy(rc.at[kinds, (z + 5 + s) % 8], rm.at[s, kinds], m_send.at[s, g], m_recv.at[s, g], z_down)

    for s in range(5):
        for g in range(2):
            kinds = slice(3 * g, 3 * g + 3)
            if s == 0:
                core_arrival(g).wait_recv()

                def add(d, _, kinds=kinds):
                    rc[kinds, d] = rc[kinds, d] + kp[kinds, d, c]
                    return 0

                lax.fori_loop(0, 8, add, 0)
            else:
                up_copy(s - 1, g).wait_recv()
                d = (z + 4 - s) % 8
                rc[kinds, d] = rc[kinds, d] + rp[s - 1, kinds]
                if s < 4:
                    down_copy(s - 1, g).wait_recv()
                    d = (z + 5 + s) % 8
                    rc[kinds, d] = rc[kinds, d] + rm[s - 1, kinds]
            if s < 4:
                up_copy(s, g).start()
            if s < 3:
                down_copy(s, g).start()

    def strip_copies(kind, cj):
        g, t = kind // 3, kind % 3
        slot = 2 * g + (t + 1) // 2
        i_y = y + (slot % 2) * (1 + slot // 2)
        i_x = jnp.where(slot == 2, 1 - xl, xl)
        j_x = jnp.where(t == 2, 1 - xl, xl)
        at_i = row_of(i_y, i_x, z // 4)
        at_j = row_of(y, j_x, cj)
        where = (xh, 2 * (z % 4) + c)
        src = fp.at[kind, cj]
        straight = ((at_i, at_j), rd.at[where], f_recv.at[0])
        turned = ((at_j, at_i), rt.at[where], f_recv.at[1])
        return src, straight, turned

    def send_strips(n, _):
        kind, cj = n // 2, n % 2
        src, straight, turned = strip_copies(kind, cj)
        for which, (to, dst, recv) in enumerate((straight, turned)):
            here = jnp.logical_and(to[0] == a, to[1] == r)
            wanted = kind >= which

            @pl.when(jnp.logical_and(wanted, here))
            def _():
                pltpu.make_async_copy(src, dst, recv).start()

            @pl.when(jnp.logical_and(wanted, jnp.logical_not(here)))
            def _():
                copy(src, dst, f_send.at[kind, cj, which], recv, to).start()

        return 0

    def wait_strips(n, _):
        kind, cj = n // 2, n % 2
        src, straight, turned = strip_copies(kind, cj)
        for which, (to, dst, recv) in enumerate((straight, turned)):
            here = jnp.logical_and(to[0] == a, to[1] == r)

            @pl.when(jnp.logical_and(kind >= which, jnp.logical_not(here)))
            def _():
                copy(src, dst, f_send.at[kind, cj, which], recv, to).wait_send()

        return 0

    for kind in range(6):
        total = rc[kind, z]
        for cj in range(2):
            fp[kind, cj] = total[:, cj * ROWS : (cj + 1) * ROWS]
    lax.fori_loop(0, 12, send_strips, 0)

    def sent(k, _):
        for j in range(3):
            to_y(k, j).wait_send()
        for j in range(4):
            for part in range(2):
                to_x(k, j, r, part).wait_send()
        for j in range(8):
            to_sibling(k, j, r).wait_send()
        to_1, to_2, to_3, to_4 = h_copies(k)
        to_1.wait_send()
        to_2.wait_send()
        pl.when(k // 2 == 1 - y // 2)(to_3.wait_send)
        pl.when(k % 2 != c)(to_4.wait_send)
        return 0

    lax.fori_loop(0, CHUNKS, sent, 0)
    for g in range(2):
        core_copy(g).wait_send()
        for s in range(4):
            up_copy(s, g).wait_send()
        for s in range(3):
            down_copy(s, g).wait_send()

    apart = (y - a // 4 + 4) % 4
    across_x = xl != (a // 2) % 2

    @pl.when(apart != 1)
    def _():
        pltpu.make_async_copy(rd, rd, f_recv.at[0]).wait()
        out[...] = (rd[0] + rd[1]).reshape(ROWS, ROWS)

    @pl.when(apart == 1)
    def _():
        out[...] = jnp.zeros_like(out)

    @pl.when(jnp.logical_and(apart != 3, jnp.logical_or(apart != 0, across_x)))
    def _():
        pltpu.make_async_copy(rt, rt, f_recv.at[1]).wait()
        out[...] = out[...] + (rt[0] + rt[1]).reshape(ROWS, ROWS).T

    lax.fori_loop(0, 12, wait_strips, 0)


def per_device(factors, orbitals, tile_mask):
    dma = pltpu.SemaphoreType.DMA
    vmem = pltpu.VMEM
    part = (SLABS, ROWS, LANES)
    return pl.pallas_call(
        kernel,
        out_shape=jax.ShapeDtypeStruct((ROWS, ROWS), F32),
        in_specs=[
            pl.BlockSpec(memory_space=pl.ANY),
            pl.BlockSpec(memory_space=pltpu.VMEM),
            pl.BlockSpec(memory_space=pltpu.SMEM),
        ],
        out_specs=pl.BlockSpec(memory_space=pltpu.VMEM),
        scratch_shapes=[
            vmem((SLABS, ROWS, 3072), F32),
            vmem((SLABS, ROWS, 3072), BF16),
            vmem((SLABS, ROWS, 3072), BF16),
            vmem((CHUNKS, 16, ROWS, LANES), F32),
            vmem((3072, 2 * LANES), BF16),
            vmem((CHUNKS, *part), F32),
            vmem((2, *part), F32),
            vmem((2, 2, *part), F32),
            vmem((2, 2, *part), F32),
            vmem((2, *part), F32),
            vmem((4, PAIR, 3 * SLABS * LANES), BF16),
            vmem((2, PAIR, 3 * SLABS * LANES), BF16),
            vmem((6, 8, 2, STRIP, PAIR), F32),
            vmem((6, 8, STRIP, PAIR), F32),
            vmem((4, 6, STRIP, PAIR), F32),
            vmem((3, 6, STRIP, PAIR), F32),
            vmem((6, 2, STRIP, ROWS), F32),
            vmem((2, 8, STRIP, ROWS), F32),
            vmem((2, 8, STRIP, ROWS), F32),
            dma((SLABS,)),
            dma((CHUNKS, 3)), dma((CHUNKS, 3)),
            dma((CHUNKS, 4, 2)), dma((CHUNKS, 4, 2)),
            dma((CHUNKS, 8)), dma((CHUNKS, 8)),
            dma((CHUNKS, 4)), dma((2,)), dma((2, 2)), dma((2, 2)), dma((2,)),
            dma((2,)), dma((2,)),
            dma((4, 2)), dma((4, 2)), dma((3, 2)), dma((3, 2)),
            dma((6, 2, 2)), dma((2,)),
        ],
        compiler_params=pltpu.CompilerParams(
            collective_id=0, has_side_effects=True, vmem_limit_bytes=60 * 2**20
        ),
    )(factors, orbitals, tile_mask)


def solution(mesh):
    placed = (P("aux", "row", None), P("row", None), P("aux", None, None))
    return jax.shard_map(
        per_device, mesh=mesh, in_specs=placed, out_specs=P("aux", "row"), check_vma=False
    )
```

```python
import jax
import jax.numpy as jnp
from jax import lax
from jax.experimental import pallas as pl
from jax.experimental.pallas import tpu as pltpu
from jax.sharding import PartitionSpec as P

F32 = jnp.float32
BF16 = jnp.bfloat16
MESH = pl.DeviceIdType.MESH
ROWS = 192
PAIR = 384
LANES = 128
CHUNKS = 4
SLABS = 3
STRIP = 48
PACK = 72
STEPS_Y = (1, -1, 2)


def split(value):
    high = value.astype(BF16)
    return high, (value - high.astype(F32)).astype(BF16)


def kernel(
    b_hbm, c_ref, mask, out,
    bf, bh, bl, cb, ch, hs, ho, hy, hx, hw, left, right, kp, rc, rp, rm, re, fp, rd, rt, ft,
    sem_b, y_send, y_recv, x_send, x_recv, s_send, s_recv,
    h_send, ho_recv, hy_recv, hx_recv, hw_recv,
    core_send, core_recv, p_send, p_recv, m_send, m_recv, e_send, e_recv, f_send, f_recv,
):
    a, r = lax.axis_index("aux"), lax.axis_index("row")
    xh, z = a // 8, a % 8
    y, xl, c = r // 4, (r // 2) % 2, r % 2
    sib = 1 - c

    def row_of(yy, xx, cc):
        return ((yy + 4) % 4 * 2 + xx) * 2 + cc

    def dev(yy, xx, cc):
        return (a, row_of(yy, xx, cc))

    def copy(src, dst, send, recv, to):
        return pltpu.make_async_remote_copy(
            src_ref=src, dst_ref=dst, send_sem=send, recv_sem=recv, device_id=to, device_id_type=MESH
        )

    across = ((a, row_of(y, 1 - xl, c)), ((1 - xh) * 8 + z, row_of(y, 1 - xl, c)))
    sibling = dev(y, xl, sib)
    z_up = (xh * 8 + (z + 1) % 8, r)
    z_down = (xh * 8 + (z + 7) % 8, r)

    slab_copies = [pltpu.make_async_copy(b_hbm.at[p], bf.at[p], sem_b.at[p]) for p in range(SLABS)]
    for each in slab_copies:
        each.start()

    barrier = pltpu.get_barrier_semaphore()
    greeted = [
        dev(y + 1, xl, c), dev(y - 1, xl, c), dev(y + 2, xl, c), across[0], across[1], sibling,
        dev(y + 1, xl, sib), dev(y, 1 - xl, sib), dev(y + 2, xl, sib), z_up, z_down,
    ]
    for each in greeted:
        pl.semaphore_signal(barrier, inc=1, device_id=each, device_id_type=MESH)
    for k in range(CHUNKS):
        cb[k, r] = c_ref[:, k * LANES : (k + 1) * LANES]
    pl.semaphore_wait(barrier, len(greeted))

    def to_y(k, j):
        return copy(cb.at[k, r], cb.at[k, r], y_send.at[k, j], y_recv.at[k, j], dev(y + STEPS_Y[j], xl, c))

    def from_y(k, j):
        block = row_of(y - STEPS_Y[j], xl, c)
        return copy(cb.at[k, block], cb.at[k, block], y_send.at[k, j], y_recv.at[k, j], sibling)

    def to_x(k, j, block, part):
        piece = cb.at[k, block, pl.ds(96 * part, 96)]
        return copy(piece, piece, x_send.at[k, j, part], x_recv.at[k, j, part], across[part])

    def to_sibling(k, j, block):
        return copy(cb.at[k, block], cb.at[k, block], s_send.at[k, j], s_recv.at[k, j], sibling)

    def y_block(j, xx, cc):
        return row_of(y - STEPS_Y[j], xx, cc) if j < 3 else row_of(y, xx, cc)

    def first(k):
        for j in range(3):
            to_y(k, j).start()
        for part in range(2):
            to_x(k, 3, r, part).start()
        to_sibling(k, 3, r).start()

    def forward_y(k):
        for j in range(3):
            from_y(k, j).wait_recv()
            block = y_block(j, xl, c)
            for part in range(2):
                to_x(k, j, block, part).start()
            to_sibling(k, j, block).start()

    def forward_x(k):
        for j in (3, 0, 1, 2):
            block = y_block(j, 1 - xl, c)
            for part in range(2):
                to_x(k, j, block, part).wait_recv()
            to_sibling(k, 4 + j, block).start()

    def whole(k):
        for j in range(4):
            to_sibling(k, j, y_block(j, xl, sib)).wait_recv()
            to_sibling(k, 4 + j, y_block(j, 1 - xl, sib)).wait_recv()

    def screen(p):
        slab_copies[p].wait()

        def tile(n, _):
            at = pl.ds(pl.multiple_of(n * LANES, LANES), LANES)
            for g in range(3):
                keep = mask[p, (3 * r + g) // 2, n].astype(F32)
                rows = pl.ds(64 * g, 64)
                high, low = split(bf[p, rows, at] * keep)
                bh[p, rows, at] = high
                bl[p, rows, at] = low
            return 0

        lax.fori_loop(0, 24, tile, 0, unroll=4)

    def half(k):
        def block(n, _):
            high, low = split(cb[k, n])
            at = pl.ds(pl.multiple_of(n * ROWS, ROWS), ROWS)
            ch[at, 0:LANES] = high
            ch[at, LANES : 2 * LANES] = low
            return 0

        lax.fori_loop(0, 16, block, 0)

        def slab(p, _):
            both = jnp.dot(bh[p], ch[...], preferred_element_type=F32)
            low = jnp.dot(bl[p], ch[:, 0:LANES], preferred_element_type=F32)
            hs[k, p] = both[:, 0:LANES] + (both[:, LANES : 2 * LANES] + low)
            return 0

        lax.fori_loop(0, SLABS, slab, 0)

    def h_copies(k):
        h, q = k % 2, k // 2
        return (
            copy(hs.at[k], hy.at[q, c], h_send.at[k, 0], hy_recv.at[q, c], dev(y - 1, xl, h)),
            copy(hs.at[k], hx.at[q, c], h_send.at[k, 1], hx_recv.at[q, c], dev(y, 1 - xl, h)),
            copy(hs.at[k], hw.at[c], h_send.at[k, 2], hw_recv.at[c], dev(y + 2, xl, h)),
            copy(hs.at[k], ho.at[q], h_send.at[k, 3], ho_recv.at[q], sibling),
        )

    def send_half(k):
        to_1, to_2, to_3, to_4 = h_copies(k)
        to_1.start()
        to_2.start()
        pl.when(k // 2 == 1 - y // 2)(to_3.start)
        pl.when(k % 2 != c)(to_4.start)

    first(0)
    first(1)
    kp[...] = jnp.zeros_like(kp)
    screen(0)
    forward_y(0)
    first(2)
    screen(1)
    forward_y(1)
    first(3)
    forward_x(0)
    screen(2)

    def step(k, _):
        @pl.when(k < CHUNKS - 2)
        def _():
            forward_y(k + 2)

        @pl.when(k < CHUNKS - 1)
        def _():
            forward_x(k + 1)

        whole(k)
        half(k)
        send_half(k)
        return 0

    lax.fori_loop(0, CHUNKS, step, 0)

    def operand(slot, core, p, value):
        rows = pl.ds(pl.multiple_of(core * ROWS, ROWS), ROWS)
        high, low = split(value)
        for where, part in ((0, high), (1, low), (2, high)):
            left[slot, rows, pl.ds((where * SLABS + p) * LANES, LANES)] = part
        if slot in (0, 2):
            for where, part in ((0, high), (1, high), (2, low)):
                right[slot // 2, rows, pl.ds((where * SLABS + p) * LANES, LANES)] = part

    def product(kind, _):
        g, t = kind // 3, kind % 3
        for core in range(2):
            value = lax.dot_general(
                left[2 * g + (t + 1) // 2],
                right[t // 2, core * ROWS : (core + 1) * ROWS],
                (((1,), (1,)), ((), ())),
                preferred_element_type=F32,
            )
            rest = value[:, LANES:ROWS].reshape(8, 2, STRIP // 2, ROWS - LANES)
            rest = jnp.concatenate([rest[:, 0], rest[:, 1]], axis=-1)
            kp[core, kind, :, 0:STRIP] += value[:, 0:LANES].reshape(8, STRIP, LANES)
            kp[core, kind, :, STRIP:PACK] += rest
        return 0

    def core_copy(g):
        kinds = pl.ds(3 * g, 3)
        return copy(kp.at[sib, kinds], rc.at[kinds], core_send.at[g], core_recv.at[g], sibling)

    def core_arrival(g):
        kinds = pl.ds(3 * g, 3)
        return copy(rc.at[kinds], rc.at[kinds], core_send.at[g], core_recv.at[g], sibling)

    def products(q, _):
        k = 2 * q + c
        copy(ho.at[q], ho.at[q], h_send.at[k, 3], ho_recv.at[q], sibling).wait_recv()
        for core in range(2):
            copy(hy.at[q, core], hy.at[q, core], h_send.at[k, 0], hy_recv.at[q, core], sibling).wait_recv()
            copy(hx.at[q, core], hx.at[q, core], h_send.at[k, 1], hx_recv.at[q, core], sibling).wait_recv()
        for p in range(SLABS):
            operand(0, c, p, hs[k, p])
            operand(0, sib, p, ho[q, p])
            for core in range(2):
                operand(1, core, p, hy[q, core, p])
                operand(2, core, p, hx[q, core, p])
        lax.fori_loop(0, 3, product, 0)

        @pl.when(q == 1)
        def _():
            core_copy(0).start()

        @pl.when(q == xl)
        def _():
            lax.fori_loop(3, 4, product, 0)

        @pl.when(q == y // 2)
        def _():
            for core in range(2):
                copy(hw.at[core], hw.at[core], h_send.at[k, 2], hw_recv.at[core], sibling).wait_recv()
            for p in range(SLABS):
                for core in range(2):
                    operand(3, core, p, hw[core, p])
            lax.fori_loop(4, 6, product, 0)

        return 0

    lax.fori_loop(0, 2, products, 0)
    core_copy(1).start()

    mine = jnp.where(xh == y // 2, 0, 1)
    groups = (1 - mine, mine)

    def kinds_of(g):
        return pl.ds(3 * g, 3)

    def up_copy(s, g):
        src = rc.at[kinds_of(g), (z + 4 - s) % 8]
        return copy(src, rp.at[s, kinds_of(g)], p_send.at[s, g], p_recv.at[s, g], z_up)

    def down_copy(s, g):
        src = rc.at[kinds_of(g), (z + 5 + s) % 8]
        return copy(src, rm.at[s, kinds_of(g)], m_send.at[s, g], m_recv.at[s, g], z_down)

    def level_copy():
        return copy(rc.at[kinds_of(1 - mine), z], re, e_send.at[0], e_recv.at[0], ((1 - xh) * 8 + z, r))

    for s in range(5):
        for n, g in enumerate(groups):
            kinds = kinds_of(g)
            if s == 0:
                core_arrival(g).wait_recv()

                def add(d, _, kinds=kinds):
                    rc[kinds, d] = rc[kinds, d] + kp[c, kinds, d]
                    return 0

                lax.fori_loop(0, 8, add, 0)
            else:
                up_copy(s - 1, g).wait_recv()
                d = (z + 4 - s) % 8
                rc[kinds, d] = rc[kinds, d] + rp[s - 1, kinds]
                if s < 4:
                    down_copy(s - 1, g).wait_recv()
                    d = (z + 5 + s) % 8
                    rc[kinds, d] = rc[kinds, d] + rm[s - 1, kinds]
            if s < 4:
                up_copy(s, g).start()
            if s < 3:
                down_copy(s, g).start()
            if s == 4 and n == 0:
                level_copy().start()

    def strip_copies(t):
        kind = 3 * mine + t
        slot = 2 * mine + (t + 1) // 2
        i_y = y + (slot % 2) * (1 + slot // 2)
        i_x = jnp.where(slot == 2, 1 - xl, xl)
        j_x = jnp.where(t == 2, 1 - xl, xl)
        at_i = row_of(i_y, i_x, z // 4)
        at_j = row_of(y, j_x, c)
        straight = ((at_i, at_j), rd.at[z % 4], f_recv.at[0])
        turned = ((at_j, at_i), rt.at[z % 4], f_recv.at[1])
        return kind, fp.at[t], straight, turned

    def send_strips(t, _):
        kind, src, straight, turned = strip_copies(t)
        for which, (to, dst, recv) in enumerate((straight, turned)):
            here = jnp.logical_and(to[0] == a, to[1] == r)
            wanted = kind >= which

            @pl.when(jnp.logical_and(wanted, here))
            def _():
                pltpu.make_async_copy(src, dst, recv).start()

            @pl.when(jnp.logical_and(wanted, jnp.logical_not(here)))
            def _():
                copy(src, dst, f_send.at[t, which], recv, to).start()

        return 0

    def wait_strips(t, _):
        kind, src, straight, turned = strip_copies(t)
        for which, (to, dst, recv) in enumerate((straight, turned)):
            here = jnp.logical_and(to[0] == a, to[1] == r)

            @pl.when(jnp.logical_and(kind >= which, jnp.logical_not(here)))
            def _():
                copy(src, dst, f_send.at[t, which], recv, to).wait_send()

        return 0

    level_copy().wait_recv()
    fp[...] = rc[kinds_of(mine), z] + re[...]
    lax.fori_loop(0, 3, send_strips, 0)

    def sent(k, _):
        for j in range(3):
            to_y(k, j).wait_send()
        for j in range(4):
            for part in range(2):
                to_x(k, j, r, part).wait_send()
        for j in range(8):
            to_sibling(k, j, r).wait_send()
        to_1, to_2, to_3, to_4 = h_copies(k)
        to_1.wait_send()
        to_2.wait_send()
        pl.when(k // 2 == 1 - y // 2)(to_3.wait_send)
        pl.when(k % 2 != c)(to_4.wait_send)
        return 0

    lax.fori_loop(0, CHUNKS, sent, 0)
    for g in range(2):
        core_copy(g).wait_send()
        for s in range(4):
            up_copy(s, g).wait_send()
        for s in range(3):
            down_copy(s, g).wait_send()

    level_copy().wait_send()

    apart = (y - a // 4 + 4) % 4
    across_x = xl != (a // 2) % 2

    def unpack(strips, block):
        for n in range(4):
            rest = strips[n, STRIP:PACK]
            at = n * STRIP
            block[at : at + STRIP, 0:LANES] = strips[n, 0:STRIP]
            block[at : at + STRIP // 2, LANES:ROWS] = rest[:, 0 : ROWS - LANES]
            block[at + STRIP // 2 : at + STRIP, LANES:ROWS] = rest[:, ROWS - LANES : LANES]

    @pl.when(apart != 1)
    def _():
        pltpu.make_async_copy(rd, rd, f_recv.at[0]).wait()
        unpack(rd, out)

    @pl.when(apart == 1)
    def _():
        out[...] = jnp.zeros_like(out)

    @pl.when(jnp.logical_and(apart != 3, jnp.logical_or(apart != 0, across_x)))
    def _():
        pltpu.make_async_copy(rt, rt, f_recv.at[1]).wait()
        unpack(rt, ft)
        out[...] = out[...] + ft[...].T

    lax.fori_loop(0, 3, wait_strips, 0)


def per_device(factors, orbitals, tile_mask):
    dma = pltpu.SemaphoreType.DMA
    vmem = pltpu.VMEM
    part = (SLABS, ROWS, LANES)
    return pl.pallas_call(
        kernel,
        out_shape=jax.ShapeDtypeStruct((ROWS, ROWS), F32),
        in_specs=[
            pl.BlockSpec(memory_space=pl.ANY),
            pl.BlockSpec(memory_space=pltpu.VMEM),
            pl.BlockSpec(memory_space=pltpu.SMEM),
        ],
        out_specs=pl.BlockSpec(memory_space=pltpu.VMEM),
        scratch_shapes=[
            vmem((SLABS, ROWS, 3072), F32),
            vmem((SLABS, ROWS, 3072), BF16),
            vmem((SLABS, ROWS, 3072), BF16),
            vmem((CHUNKS, 16, ROWS, LANES), F32),
            vmem((3072, 2 * LANES), BF16),
            vmem((CHUNKS, *part), F32),
            vmem((2, *part), F32),
            vmem((2, 2, *part), F32),
            vmem((2, 2, *part), F32),
            vmem((2, *part), F32),
            vmem((4, PAIR, 3 * SLABS * LANES), BF16),
            vmem((2, PAIR, 3 * SLABS * LANES), BF16),
            vmem((2, 6, 8, PACK, LANES), F32),
            vmem((6, 8, PACK, LANES), F32),
            vmem((4, 6, PACK, LANES), F32),
            vmem((3, 6, PACK, LANES), F32),
            vmem((3, PACK, LANES), F32),
            vmem((3, PACK, LANES), F32),
            vmem((4, PACK, LANES), F32),
            vmem((4, PACK, LANES), F32),
            vmem((ROWS, ROWS), F32),
            dma((SLABS,)),
            dma((CHUNKS, 3)), dma((CHUNKS, 3)),
            dma((CHUNKS, 4, 2)), dma((CHUNKS, 4, 2)),
            dma((CHUNKS, 8)), dma((CHUNKS, 8)),
            dma((CHUNKS, 4)), dma((2,)), dma((2, 2)), dma((2, 2)), dma((2,)),
            dma((2,)), dma((2,)),
            dma((4, 2)), dma((4, 2)), dma((3, 2)), dma((3, 2)),
            dma((1,)), dma((1,)),
            dma((3, 2)), dma((2,)),
        ],
        compiler_params=pltpu.CompilerParams(
            collective_id=0, has_side_effects=True, vmem_limit_bytes=60 * 2**20
        ),
    )(factors, orbitals, tile_mask)


def solution(mesh):
    placed = (P("aux", "row", None), P("row", None), P("aux", None, None))
    return jax.shard_map(
        per_device, mesh=mesh, in_specs=placed, out_specs=P("aux", "row"), check_vma=False
    )
```

```python
import jax
import jax.numpy as jnp
from jax import lax
from jax.experimental import pallas as pl
from jax.experimental.pallas import tpu as pltpu
from jax.sharding import PartitionSpec as P

F32 = jnp.float32
BF16 = jnp.bfloat16
MESH = pl.DeviceIdType.MESH
ROWS = 192
PAIR = 384
LANES = 128
CHUNKS = 4
PLANE = 2
SLICE = 24
SLABS = 3
STRIP = 48
PACK = 72
STEPS_Y = (1, -1, 2)


def split(value):
    high = value.astype(BF16)
    return high, (value - high.astype(F32)).astype(BF16)


def kernel(
    b_hbm, c_ref, mask, out,
    bf, bh, bl, cb, ch, hs, ho, hy, hx, hw, wr, left, right, kp, rc, rp, rm, re, fp, rd, rt, ft,
    sem_b, y_send, y_recv, x_send, x_recv, s_send, s_recv,
    g_send, g_recv, long_send, long_recv, short_send, short_recv, zs_send, zs_recv,
    h_send, ho_recv, hy_recv, hx_recv, hw_recv, wr_send, wr_recv,
    core_send, core_recv, p_send, p_recv, m_send, m_recv, e_send, e_recv, f_send, f_recv,
):
    a, r = lax.axis_index("aux"), lax.axis_index("row")
    xh, z = a // 8, a % 8
    y, xl, c = r // 4, (r // 2) % 2, r % 2
    sib = 1 - c

    def row_of(yy, xx, cc):
        return ((yy + 4) % 4 * 2 + xx) * 2 + cc

    def dev(yy, xx, cc):
        return (a, row_of(yy, xx, cc))

    def copy(src, dst, send, recv, to):
        return pltpu.make_async_remote_copy(
            src_ref=src, dst_ref=dst, send_sem=send, recv_sem=recv, device_id=to, device_id_type=MESH
        )

    across = ((a, row_of(y, 1 - xl, c)), ((1 - xh) * 8 + z, row_of(y, 1 - xl, c)))
    sibling = dev(y, xl, sib)
    z_up = (xh * 8 + (z + 1) % 8, r)
    z_down = (xh * 8 + (z + 7) % 8, r)

    slab_copies = [pltpu.make_async_copy(b_hbm.at[p], bf.at[p], sem_b.at[p]) for p in range(SLABS)]
    for each in slab_copies:
        each.start()

    here = 2 * y + xl
    for k in range(CHUNKS):
        cb[k, c, here] = c_ref[:, k * LANES : (k + 1) * LANES]

    barrier = pltpu.get_barrier_semaphore()
    peers = [dev(y + dy, xl, c) for dy in STEPS_Y] + [dev(y + dy, 1 - xl, c) for dy in (0, *STEPS_Y)]
    greeted = [
        *peers, across[1], sibling, z_up, z_down,
    ]
    for each in greeted:
        pl.semaphore_signal(barrier, inc=1, device_id=each, device_id_type=MESH)
    pl.semaphore_wait(barrier, len(greeted))

    def place(yy, xx):
        return (yy + 4) % 4 * 2 + xx

    def to_y(k, j):
        block = cb.at[k, c, here]
        return copy(block, block, y_send.at[k, j], y_recv.at[k, j], dev(y + STEPS_Y[j], xl, c))

    def from_y(k, j):
        block = cb.at[k, c, place(y - STEPS_Y[j], xl)]
        return copy(block, block, y_send.at[k, j], y_recv.at[k, j], sibling)

    def to_x(k, j, at, part):
        piece = cb.at[k, c, at, pl.ds(96 * part, 96)]
        return copy(piece, piece, x_send.at[k, j, part], x_recv.at[k, j, part], across[part])

    def to_sibling(k, j, at, core):
        block = cb.at[k, core, at]
        return copy(block, block, s_send.at[k, j], s_recv.at[k, j], sibling)

    def y_place(j, xx):
        return place(y - STEPS_Y[j], xx) if j < 3 else place(y, xx)

    def first(k):
        for j in range(3):
            to_y(k, j).start()
        for part in range(2):
            to_x(k, 3, here, part).start()
        to_sibling(k, 3, here, c).start()

    def forward_y(k):
        for j in range(3):
            from_y(k, j).wait_recv()
            at = y_place(j, xl)
            for part in range(2):
                to_x(k, j, at, part).start()
            to_sibling(k, j, at, c).start()

    def forward_x(k):
        for j in (3, 0, 1, 2):
            at = y_place(j, 1 - xl)
            for part in range(2):
                to_x(k, j, at, part).wait_recv()
            to_sibling(k, 4 + j, at, c).start()

    def slices(j, at):
        piece = cb.at[pl.ds(PLANE, CHUNKS - PLANE), c, at, pl.ds(SLICE * z, SLICE)]
        return copy(piece, piece, g_send.at[j], g_recv.at[j], peers[j])

    far = 1 - 2 * c
    z_far = (xh * 8 + (z + 8 + far) % 8, r)
    z_near = (xh * 8 + (z + 8 - far) % 8, r)

    def z_piece(k, core, at):
        return cb.at[k, core, :, pl.ds(SLICE * ((z + 8 + at) % 8), SLICE)]

    def to_far(k, s):
        piece = z_piece(k, c, -far * s)
        return copy(piece, piece, long_send.at[k, s], long_recv.at[k, s], z_far)

    def from_far(k, s):
        piece = z_piece(k, c, -far * (s + 1))
        return copy(piece, piece, long_send.at[k, s], long_recv.at[k, s], z_far)

    def to_near(k, s):
        piece = z_piece(k, c, far * s)
        return copy(piece, piece, short_send.at[k, s], short_recv.at[k, s], z_near)

    def from_near(k, s):
        piece = z_piece(k, c, far * (s + 1))
        return copy(piece, piece, short_send.at[k, s], short_recv.at[k, s], z_near)

    def z_sibling(k, core, j):
        piece = z_piece(k, core, j)
        at = (j + 8) % 8
        return copy(piece, piece, zs_send.at[k, at], zs_recv.at[k, at], sibling)

    def plane_slices():
        for j in range(7):
            slices(j, here).start()

    def z_first():
        for j in range(7):
            at = place(y - STEPS_Y[j], xl) if j < 3 else place(y, 1 - xl) if j == 3 else place(y - STEPS_Y[j - 4], 1 - xl)
            slices(j, at).wait_recv()

    def z_own(k):
        to_far(k, 0).start()
        to_near(k, 0).start()
        z_sibling(k, c, 0).start()

    def z_step(k, s):
        from_far(k, s).wait_recv()
        if s < 3:
            to_far(k, s + 1).start()
        z_sibling(k, c, -far * (s + 1)).start()
        if s < 3:
            from_near(k, s).wait_recv()
            if s < 2:
                to_near(k, s + 1).start()
            z_sibling(k, c, far * (s + 1)).start()

    def whole(k):
        if k < PLANE:
            for j in range(4):
                to_sibling(k, j, y_place(j, xl), sib).wait_recv()
                to_sibling(k, 4 + j, y_place(j, 1 - xl), sib).wait_recv()
        else:
            for j in range(8):
                z_sibling(k, sib, j).wait_recv()

    def screen(p):
        slab_copies[p].wait()

        def tile(n, _):
            at = pl.ds(pl.multiple_of(n * LANES, LANES), LANES)
            for g in range(3):
                keep = mask[p, (3 * r + g) // 2, n].astype(F32)
                rows = pl.ds(64 * g, 64)
                high, low = split(bf[p, rows, at] * keep)
                bh[p, rows, at] = high
                bl[p, rows, at] = low
            return 0

        lax.fori_loop(0, 24, tile, 0, unroll=4)

    def half(k):
        def block(n, _):
            high, low = split(cb[k, n % 2, n // 2])
            at = pl.ds(pl.multiple_of(n * ROWS, ROWS), ROWS)
            ch[at, 0:LANES] = high
            ch[at, LANES : 2 * LANES] = low
            return 0

        lax.fori_loop(0, 16, block, 0)

        def slab(p, _):
            both = jnp.dot(bh[p], ch[...], preferred_element_type=F32)
            low = jnp.dot(bl[p], ch[:, 0:LANES], preferred_element_type=F32)
            hs[k, p] = both[:, 0:LANES] + (both[:, LANES : 2 * LANES] + low)
            return 0

        lax.fori_loop(0, SLABS, slab, 0)

    def h_copies(k):
        h, q = k % 2, k // 2
        return (
            copy(hs.at[k], hy.at[q, c], h_send.at[k, 0], hy_recv.at[q, c], dev(y - 1, xl, h)),
            copy(hs.at[k], hx.at[q, c], h_send.at[k, 1], hx_recv.at[q, c], dev(y, 1 - xl, h)),
            copy(hs.at[k], wr.at[h], h_send.at[k, 2], wr_recv.at[h], dev(y + 1, xl, c)),
            copy(hs.at[k], ho.at[q], h_send.at[k, 3], ho_recv.at[q], sibling),
        )

    def send_half(k):
        to_1, to_2, to_3, to_4 = h_copies(k)
        to_1.start()
        to_2.start()
        pl.when(k // 2 == 1 - y // 2)(to_3.start)
        pl.when(k % 2 != c)(to_4.start)

    def relay_copy(k):
        h = k % 2
        return copy(wr.at[h], hw.at[c], wr_send.at[h], hw_recv.at[c], dev(y + 1, xl, h))

    def relays(k):
        return k // 2 == 1 - (y + 3) % 4 // 2

    def relay(k):
        @pl.when(relays(k))
        def _():
            h = k % 2
            copy(wr.at[h], wr.at[h], wr_send.at[h], wr_recv.at[h], sibling).wait_recv()
            relay_copy(k).start()

    plane_slices()
    first(0)
    kp[...] = jnp.zeros_like(kp)
    screen(0)
    z_first()
    z_own(2)
    forward_y(0)
    first(1)
    screen(1)
    z_step(2, 0)
    forward_x(0)
    forward_y(1)
    z_own(3)
    screen(2)
    z_step(2, 1)
    whole(0)
    half(0)
    send_half(0)
    forward_x(1)
    z_step(2, 2)
    z_step(3, 0)
    whole(1)
    half(1)
    send_half(1)
    z_step(2, 3)
    z_step(3, 1)
    whole(2)
    half(2)
    send_half(2)
    z_step(3, 2)
    z_step(3, 3)
    relay(0)
    relay(1)
    whole(3)
    half(3)
    send_half(3)
    relay(2)

    def operand(slot, core, p, value):
        rows = pl.ds(pl.multiple_of(core * ROWS, ROWS), ROWS)
        high, low = split(value)
        for where, part in ((0, high), (1, low), (2, high)):
            left[slot, rows, pl.ds((where * SLABS + p) * LANES, LANES)] = part
        if slot in (0, 2):
            for where, part in ((0, high), (1, high), (2, low)):
                right[slot // 2, rows, pl.ds((where * SLABS + p) * LANES, LANES)] = part

    def product(kind):
        rows, columns = ((0, 0), (1, 1), (1, 0), (2, 0), (3, 0), (3, 1))[kind]

        def one(core, _):
            at = pl.ds(pl.multiple_of(core * ROWS, ROWS), ROWS)
            value = lax.dot_general(
                left[rows], right[columns, at], (((1,), (1,)), ((), ())), preferred_element_type=F32
            )
            rest = value[:, LANES:ROWS].reshape(8, 2, STRIP // 2, ROWS - LANES)
            rest = jnp.concatenate([rest[:, 0], rest[:, 1]], axis=-1)
            kp[core, kind, :, 0:STRIP] += value[:, 0:LANES].reshape(8, STRIP, LANES)
            kp[core, kind, :, STRIP:PACK] += rest
            return 0

        lax.fori_loop(0, 2, one, 0)

    def kinds_of(g):
        start, count = ((0, 1), (1, 3), (4, 2))[g]
        return pl.ds(start, count)

    def core_copy(g):
        kinds = kinds_of(g)
        return copy(kp.at[sib, kinds], rc.at[kinds], core_send.at[g], core_recv.at[g], sibling)

    def core_arrival(g):
        kinds = kinds_of(g)
        return copy(rc.at[kinds], rc.at[kinds], core_send.at[g], core_recv.at[g], sibling)

    def take_o(q):
        copy(ho.at[q], ho.at[q], h_send.at[2 * q + c, 3], ho_recv.at[q], sibling).wait_recv()
        for p in range(SLABS):
            operand(0, c, p, hs[2 * q + c, p])
            operand(0, sib, p, ho[q, p])

    def take_y_x(q):
        k = 2 * q + c
        for core in range(2):
            copy(hy.at[q, core], hy.at[q, core], h_send.at[k, 0], hy_recv.at[q, core], sibling).wait_recv()
            copy(hx.at[q, core], hx.at[q, core], h_send.at[k, 1], hx_recv.at[q, core], sibling).wait_recv()
        for p in range(SLABS):
            for core in range(2):
                operand(1, core, p, hy[q, core, p])
                operand(2, core, p, hx[q, core, p])

    def products_y_x(q):
        product(1)
        product(2)
        pl.when(xl == q)(lambda: product(3))

    def products_w(q):
        @pl.when(y // 2 == q)
        def _():
            for core in range(2):
                copy(hw.at[core], hw.at[core], wr_send.at[core], hw_recv.at[core], sibling).wait_recv()
            for p in range(SLABS):
                for core in range(2):
                    operand(3, core, p, hw[core, p])
            product(4)
            product(5)

    mine = jnp.where(xh == y // 2, 0, 1)

    def up_copy(s, g):
        src = rc.at[kinds_of(g), (z + 4 - s) % 8]
        return copy(src, rp.at[s, kinds_of(g)], p_send.at[s, g], p_recv.at[s, g], z_up)

    def down_copy(s, g):
        src = rc.at[kinds_of(g), (z + 5 + s) % 8]
        return copy(src, rm.at[s, kinds_of(g)], m_send.at[s, g], m_recv.at[s, g], z_down)

    def sum_step(s, g):
        kinds = kinds_of(g)
        if s == 0:
            core_arrival(g).wait_recv()

            def add(d, _):
                rc[kinds, d] = rc[kinds, d] + kp[c, kinds, d]
                return 0

            lax.fori_loop(0, 8, add, 0)
        else:
            up_copy(s - 1, g).wait_recv()
            d = (z + 4 - s) % 8
            rc[kinds, d] = rc[kinds, d] + rp[s - 1, kinds]
            if s < 4:
                down_copy(s - 1, g).wait_recv()
                d = (z + 5 + s) % 8
                rc[kinds, d] = rc[kinds, d] + rm[s - 1, kinds]
        if s < 4:
            up_copy(s, g).start()
        if s < 3:
            down_copy(s, g).start()

    def level_copy(t):
        src = rc.at[2 * t + 1 - mine, z]
        return copy(src, re.at[t], e_send.at[t], e_recv.at[t], ((1 - xh) * 8 + z, r))

    def strip_copies(t):
        i_y = y + (mine, 1 - mine, 2)[t]
        i_x = (xl + mine) % 2 if t == 1 else xl
        j_x = xl if t == 1 else (xl + mine) % 2
        at_i = row_of(i_y, i_x, z // 4)
        at_j = row_of(y, j_x, c)
        straight = ((at_i, at_j), rd.at[z % 4], f_recv.at[0])
        turned = ((at_j, at_i), rt.at[z % 4], f_recv.at[1])
        return straight, turned

    def hand_out(t):
        level_copy(t).wait_recv()
        fp[t] = rc[2 * t + mine, z] + re[t]
        for which, (to, dst, recv) in enumerate(strip_copies(t)):
            own = jnp.logical_and(to[0] == a, to[1] == r)
            wanted = 2 * t + mine >= which

            @pl.when(jnp.logical_and(wanted, own))
            def _(dst=dst, recv=recv):
                pltpu.make_async_copy(fp.at[t], dst, recv).start()

            @pl.when(jnp.logical_and(wanted, jnp.logical_not(own)))
            def _(dst=dst, recv=recv, to=to, which=which):
                copy(fp.at[t], dst, f_send.at[t, which], recv, to).start()

    def handed_out(t):
        for which, (to, dst, recv) in enumerate(strip_copies(t)):
            own = jnp.logical_and(to[0] == a, to[1] == r)

            @pl.when(jnp.logical_and(2 * t + mine >= which, jnp.logical_not(own)))
            def _(dst=dst, recv=recv, to=to, which=which):
                copy(fp.at[t], dst, f_send.at[t, which], recv, to).wait_send()

    take_o(0)
    product(0)
    take_y_x(0)
    products_y_x(0)
    products_w(0)
    relay(3)
    take_o(1)
    product(0)
    core_copy(0).start()
    take_y_x(1)
    products_y_x(1)
    core_copy(1).start()
    sum_step(0, 0)
    sum_step(0, 1)
    sum_step(1, 0)
    sum_step(1, 1)
    products_w(1)
    core_copy(2).start()
    sum_step(2, 0)
    sum_step(2, 1)
    sum_step(0, 2)
    sum_step(3, 0)
    sum_step(3, 1)
    sum_step(1, 2)
    sum_step(4, 0)
    sum_step(4, 1)
    level_copy(0).start()
    level_copy(1).start()
    sum_step(2, 2)
    hand_out(0)
    hand_out(1)
    sum_step(3, 2)
    sum_step(4, 2)
    level_copy(2).start()
    hand_out(2)

    def sent(k, _):
        to_1, to_2, to_3, to_4 = h_copies(k)
        to_1.wait_send()
        to_2.wait_send()
        pl.when(k // 2 == 1 - y // 2)(to_3.wait_send)
        pl.when(k % 2 != c)(to_4.wait_send)
        pl.when(relays(k))(relay_copy(k).wait_send)
        return 0

    def sent_plane(k, _):
        for j in range(3):
            to_y(k, j).wait_send()
        for j in range(4):
            for part in range(2):
                to_x(k, j, here, part).wait_send()
        for j in range(8):
            to_sibling(k, j, here, c).wait_send()
        return 0

    def sent_z(k, _):
        for s in range(4):
            to_far(k, s).wait_send()
        for s in range(3):
            to_near(k, s).wait_send()
        for j in range(8):
            z_sibling(k, c, j).wait_send()
        return 0

    lax.fori_loop(0, CHUNKS, sent, 0)
    lax.fori_loop(0, PLANE, sent_plane, 0)
    lax.fori_loop(PLANE, CHUNKS, sent_z, 0)
    for j in range(7):
        slices(j, here).wait_send()
    for g in range(3):
        core_copy(g).wait_send()
        for s in range(4):
            up_copy(s, g).wait_send()
        for s in range(3):
            down_copy(s, g).wait_send()

    for t in range(3):
        level_copy(t).wait_send()

    apart = (y - a // 4 + 4) % 4
    across_x = xl != (a // 2) % 2

    def unpack(strips, block):
        for n in range(4):
            rest = strips[n, STRIP:PACK]
            at = n * STRIP
            block[at : at + STRIP, 0:LANES] = strips[n, 0:STRIP]
            block[at : at + STRIP // 2, LANES:ROWS] = rest[:, 0 : ROWS - LANES]
            block[at + STRIP // 2 : at + STRIP, LANES:ROWS] = rest[:, ROWS - LANES : LANES]

    @pl.when(apart != 1)
    def _():
        pltpu.make_async_copy(rd, rd, f_recv.at[0]).wait()
        unpack(rd, out)

    @pl.when(apart == 1)
    def _():
        out[...] = jnp.zeros_like(out)

    @pl.when(jnp.logical_and(apart != 3, jnp.logical_or(apart != 0, across_x)))
    def _():
        pltpu.make_async_copy(rt, rt, f_recv.at[1]).wait()
        unpack(rt, ft)
        out[...] = out[...] + ft[...].T

    for t in range(3):
        handed_out(t)


def per_device(factors, orbitals, tile_mask):
    dma = pltpu.SemaphoreType.DMA
    vmem = pltpu.VMEM
    part = (SLABS, ROWS, LANES)
    return pl.pallas_call(
        kernel,
        out_shape=jax.ShapeDtypeStruct((ROWS, ROWS), F32),
        in_specs=[
            pl.BlockSpec(memory_space=pl.ANY),
            pl.BlockSpec(memory_space=pltpu.VMEM),
            pl.BlockSpec(memory_space=pltpu.SMEM),
        ],
        out_specs=pl.BlockSpec(memory_space=pltpu.VMEM),
        scratch_shapes=[
            vmem((SLABS, ROWS, 3072), F32),
            vmem((SLABS, ROWS, 3072), BF16),
            vmem((SLABS, ROWS, 3072), BF16),
            vmem((CHUNKS, 2, 8, ROWS, LANES), F32),
            vmem((3072, 2 * LANES), BF16),
            vmem((CHUNKS, *part), F32),
            vmem((2, *part), F32),
            vmem((2, 2, *part), F32),
            vmem((2, 2, *part), F32),
            vmem((2, *part), F32),
            vmem((2, *part), F32),
            vmem((4, PAIR, 3 * SLABS * LANES), BF16),
            vmem((2, PAIR, 3 * SLABS * LANES), BF16),
            vmem((2, 6, 8, PACK, LANES), F32),
            vmem((6, 8, PACK, LANES), F32),
            vmem((4, 6, PACK, LANES), F32),
            vmem((3, 6, PACK, LANES), F32),
            vmem((3, PACK, LANES), F32),
            vmem((3, PACK, LANES), F32),
            vmem((4, PACK, LANES), F32),
            vmem((4, PACK, LANES), F32),
            vmem((ROWS, ROWS), F32),
            dma((SLABS,)),
            dma((CHUNKS, 3)), dma((CHUNKS, 3)),
            dma((CHUNKS, 4, 2)), dma((CHUNKS, 4, 2)),
            dma((CHUNKS, 8)), dma((CHUNKS, 8)),
            dma((7,)), dma((7,)), dma((CHUNKS, 4)), dma((CHUNKS, 4)), dma((CHUNKS, 3)), dma((CHUNKS, 3)),
            dma((CHUNKS, 8)), dma((CHUNKS, 8)),
            dma((CHUNKS, 4)), dma((2,)), dma((2, 2)), dma((2, 2)), dma((2,)), dma((2,)), dma((2,)),
            dma((3,)), dma((3,)),
            dma((4, 3)), dma((4, 3)), dma((3, 3)), dma((3, 3)),
            dma((3,)), dma((3,)),
            dma((3, 2)), dma((2,)),
        ],
        compiler_params=pltpu.CompilerParams(
            collective_id=0, has_side_effects=True, vmem_limit_bytes=60 * 2**20
        ),
    )(factors, orbitals, tile_mask)


def solution(mesh):
    placed = (P("aux", "row", None), P("row", None), P("aux", None, None))
    return jax.shard_map(
        per_device, mesh=mesh, in_specs=placed, out_specs=P("aux", "row"), check_vma=False
    )
```

```python
import jax
import jax.numpy as jnp
from jax import lax
from jax.experimental import pallas as pl
from jax.experimental.pallas import tpu as pltpu
from jax.sharding import PartitionSpec as P

F32 = jnp.float32
BF16 = jnp.bfloat16
MESH = pl.DeviceIdType.MESH
ROWS = 192
PAIR = 384
LANES = 128
CHUNKS = 4
PLANE = 2
SLICE = 24
SLABS = 3
STRIP = 48
PACK = 72
STEPS_Y = (1, -1, 2)


def split(value):
    high = value.astype(BF16)
    return high, (value - high.astype(F32)).astype(BF16)


def kernel(
    b_hbm, c_ref, mask, out,
    bf, bh, bl, cb, ch, hs, ho, hy, hx, hw, wr, left, right, kp, rc, rp, rm, re, fp, rd, rt, ft,
    sem_b, y_send, y_recv, x_send, x_recv, s_send, s_recv,
    g_send, g_recv, long_send, long_recv, short_send, short_recv, zs_send, zs_recv,
    h_send, w_send, ho_recv, hy_recv, hx_recv, hw_recv, wr_send, wr_recv,
    core_send, core_recv, p_send, p_recv, m_send, m_recv, e_send, e_recv, f_send, f_recv,
):
    a, r = lax.axis_index("aux"), lax.axis_index("row")
    xh, z = a // 8, a % 8
    y, xl, c = r // 4, (r // 2) % 2, r % 2
    sib = 1 - c

    def row_of(yy, xx, cc):
        return ((yy + 4) % 4 * 2 + xx) * 2 + cc

    def dev(yy, xx, cc):
        return (a, row_of(yy, xx, cc))

    def copy(src, dst, send, recv, to):
        return pltpu.make_async_remote_copy(
            src_ref=src, dst_ref=dst, send_sem=send, recv_sem=recv, device_id=to, device_id_type=MESH
        )

    across = ((a, row_of(y, 1 - xl, c)), ((1 - xh) * 8 + z, row_of(y, 1 - xl, c)))
    sibling = dev(y, xl, sib)
    z_up = (xh * 8 + (z + 1) % 8, r)
    z_down = (xh * 8 + (z + 7) % 8, r)

    slab_copies = [pltpu.make_async_copy(b_hbm.at[p], bf.at[p], sem_b.at[p]) for p in range(SLABS)]
    for each in slab_copies:
        each.start()

    here = 2 * y + xl
    for k in range(CHUNKS):
        cb[k, c, here] = c_ref[:, k * LANES : (k + 1) * LANES]

    barrier = pltpu.get_barrier_semaphore()
    peers = [dev(y + dy, xl, c) for dy in STEPS_Y] + [dev(y + dy, 1 - xl, c) for dy in (0, *STEPS_Y)]
    greeted = [
        *peers, across[1], sibling, z_up, z_down,
    ]
    for each in greeted:
        pl.semaphore_signal(barrier, inc=1, device_id=each, device_id_type=MESH)
    pl.semaphore_wait(barrier, len(greeted))

    def place(yy, xx):
        return (yy + 4) % 4 * 2 + xx

    def to_y(k, j):
        block = cb.at[k, c, here]
        return copy(block, block, y_send.at[k, j], y_recv.at[k, j], dev(y + STEPS_Y[j], xl, c))

    def from_y(k, j):
        block = cb.at[k, c, place(y - STEPS_Y[j], xl)]
        return copy(block, block, y_send.at[k, j], y_recv.at[k, j], sibling)

    def to_x(k, j, at, part):
        piece = cb.at[k, c, at, pl.ds(96 * part, 96)]
        return copy(piece, piece, x_send.at[k, j, part], x_recv.at[k, j, part], across[part])

    def to_sibling(k, j, at, core):
        block = cb.at[k, core, at]
        return copy(block, block, s_send.at[k, j], s_recv.at[k, j], sibling)

    def y_place(j, xx):
        return place(y - STEPS_Y[j], xx) if j < 3 else place(y, xx)

    def first(k):
        for j in range(3):
            to_y(k, j).start()
        for part in range(2):
            to_x(k, 3, here, part).start()
        to_sibling(k, 3, here, c).start()

    def forward_y(k):
        for j in range(3):
            from_y(k, j).wait_recv()
            at = y_place(j, xl)
            for part in range(2):
                to_x(k, j, at, part).start()
            to_sibling(k, j, at, c).start()

    def forward_x(k):
        for j in (3, 0, 1, 2):
            at = y_place(j, 1 - xl)
            for part in range(2):
                to_x(k, j, at, part).wait_recv()
            to_sibling(k, 4 + j, at, c).start()

    def slices(j, at):
        piece = cb.at[pl.ds(PLANE, CHUNKS - PLANE), c, at, pl.ds(SLICE * z, SLICE)]
        return copy(piece, piece, g_send.at[j], g_recv.at[j], peers[j])

    far = 1 - 2 * c
    z_far = (xh * 8 + (z + 8 + far) % 8, r)
    z_near = (xh * 8 + (z + 8 - far) % 8, r)

    def z_piece(k, core, at):
        return cb.at[k, core, :, pl.ds(SLICE * ((z + 8 + at) % 8), SLICE)]

    def to_far(k, s):
        piece = z_piece(k, c, -far * s)
        return copy(piece, piece, long_send.at[k, s], long_recv.at[k, s], z_far)

    def from_far(k, s):
        piece = z_piece(k, c, -far * (s + 1))
        return copy(piece, piece, long_send.at[k, s], long_recv.at[k, s], z_far)

    def to_near(k, s):
        piece = z_piece(k, c, far * s)
        return copy(piece, piece, short_send.at[k, s], short_recv.at[k, s], z_near)

    def from_near(k, s):
        piece = z_piece(k, c, far * (s + 1))
        return copy(piece, piece, short_send.at[k, s], short_recv.at[k, s], z_near)

    def z_sibling(k, core, j):
        piece = z_piece(k, core, j)
        at = (j + 8) % 8
        return copy(piece, piece, zs_send.at[k, at], zs_recv.at[k, at], sibling)

    def plane_slices():
        for j in range(7):
            slices(j, here).start()

    def z_first():
        for j in range(7):
            at = place(y - STEPS_Y[j], xl) if j < 3 else place(y, 1 - xl) if j == 3 else place(y - STEPS_Y[j - 4], 1 - xl)
            slices(j, at).wait_recv()

    def z_own(k):
        to_far(k, 0).start()
        to_near(k, 0).start()
        z_sibling(k, c, 0).start()

    def z_step(k, s):
        from_far(k, s).wait_recv()
        if s < 3:
            to_far(k, s + 1).start()
        z_sibling(k, c, -far * (s + 1)).start()
        if s < 3:
            from_near(k, s).wait_recv()
            if s < 2:
                to_near(k, s + 1).start()
            z_sibling(k, c, far * (s + 1)).start()

    def whole(k):
        if k < PLANE:
            for j in range(4):
                to_sibling(k, j, y_place(j, xl), sib).wait_recv()
                to_sibling(k, 4 + j, y_place(j, 1 - xl), sib).wait_recv()
        else:
            for j in range(8):
                z_sibling(k, sib, j).wait_recv()

    def screen(p):
        slab_copies[p].wait()

        def tile(n, _):
            at = pl.ds(pl.multiple_of(n * LANES, LANES), LANES)
            for g in range(3):
                keep = mask[p, (3 * r + g) // 2, n].astype(F32)
                rows = pl.ds(64 * g, 64)
                high, low = split(bf[p, rows, at] * keep)
                bh[p, rows, at] = high
                bl[p, rows, at] = low
            return 0

        lax.fori_loop(0, 24, tile, 0, unroll=4)

    def half(k):
        def block(n, _):
            high, low = split(cb[k, n % 2, n // 2])
            at = pl.ds(pl.multiple_of(n * ROWS, ROWS), ROWS)
            ch[at, 0:LANES] = high
            ch[at, LANES : 2 * LANES] = low
            return 0

        lax.fori_loop(0, 16, block, 0)

        def slab(p, _):
            both = jnp.dot(bh[p], ch[...], preferred_element_type=F32)
            low = jnp.dot(bl[p], ch[:, 0:LANES], preferred_element_type=F32)
            hs[k, p] = both[:, 0:LANES] + (both[:, LANES : 2 * LANES] + low)
            return 0

        lax.fori_loop(0, SLABS, slab, 0)

    def h_copies(k):
        h, q = k % 2, k // 2
        return (
            copy(hs.at[k], hy.at[q, c], h_send.at[k, 0], hy_recv.at[q, c], dev(y - 1, xl, h)),
            copy(hs.at[k], hx.at[q, c], h_send.at[k, 1], hx_recv.at[q, c], dev(y, 1 - xl, h)),
            copy(hs.at[k], ho.at[q], h_send.at[k, 2], ho_recv.at[q], sibling),
        )

    def w_copy(k, p):
        h = k % 2
        return copy(hs.at[k, p], wr.at[h, p], w_send.at[k, p], wr_recv.at[h, p], dev(y + 1, xl, c))

    def w_half(yy, core):
        return ((yy + 4) % 4 // 2 + core) % 2

    def sends_w(k):
        return k // 2 == w_half(y + 2, k % 2)

    def send_half(k):
        to_1, to_2, to_3 = h_copies(k)

        @pl.when(sends_w(k))
        def _():
            for p in range(SLABS):
                w_copy(k, p).start()

        to_1.start()
        to_2.start()
        pl.when(k % 2 != c)(to_3.start)

    def relay_copy(k, p):
        h = k % 2
        return copy(wr.at[h, p], hw.at[c, p], wr_send.at[h, p], hw_recv.at[c, p], dev(y + 1, xl, h))

    def relays(k):
        return k // 2 == w_half(y + 1, k % 2)

    def relay(k, slabs=range(SLABS)):
        @pl.when(relays(k))
        def _():
            h = k % 2
            for p in slabs:
                copy(wr.at[h, p], wr.at[h, p], wr_send.at[h, p], wr_recv.at[h, p], sibling).wait_recv()
                relay_copy(k, p).start()

    plane_slices()
    first(0)
    kp[...] = jnp.zeros_like(kp)
    screen(0)
    z_first()
    z_own(2)
    forward_y(0)
    first(1)
    screen(1)
    z_step(2, 0)
    forward_x(0)
    forward_y(1)
    z_own(3)
    screen(2)
    z_step(2, 1)
    whole(0)
    half(0)
    send_half(0)
    forward_x(1)
    z_step(2, 2)
    z_step(3, 0)
    whole(1)
    half(1)
    send_half(1)
    z_step(2, 3)
    z_step(3, 1)
    whole(2)
    half(2)
    send_half(2)
    z_step(3, 2)
    z_step(3, 3)
    relay(0)
    relay(1)
    whole(3)
    half(3)
    send_half(3)

    def operand(slot, core, p, value):
        rows = pl.ds(pl.multiple_of(core * ROWS, ROWS), ROWS)
        high, low = split(value)
        for where, part in ((0, high), (1, low), (2, high)):
            left[slot, rows, pl.ds((where * SLABS + p) * LANES, LANES)] = part
        if slot in (0, 2):
            for where, part in ((0, high), (1, high), (2, low)):
                right[slot // 2, rows, pl.ds((where * SLABS + p) * LANES, LANES)] = part

    def product(kind):
        rows, columns = ((0, 0), (1, 1), (1, 0), (2, 0), (3, 0), (3, 1))[kind]

        def one(core, _):
            at = pl.ds(pl.multiple_of(core * ROWS, ROWS), ROWS)
            value = lax.dot_general(
                left[rows], right[columns, at], (((1,), (1,)), ((), ())), preferred_element_type=F32
            )
            rest = value[:, LANES:ROWS].reshape(8, 2, STRIP // 2, ROWS - LANES)
            rest = jnp.concatenate([rest[:, 0], rest[:, 1]], axis=-1)
            kp[core, kind, :, 0:STRIP] += value[:, 0:LANES].reshape(8, STRIP, LANES)
            kp[core, kind, :, STRIP:PACK] += rest
            return 0

        lax.fori_loop(0, 2, one, 0)

    def kinds_of(g):
        start, count = ((0, 1), (1, 1), (2, 2), (4, 1), (5, 1))[g]
        return pl.ds(start, count)

    def core_copy(g):
        kinds = kinds_of(g)
        return copy(kp.at[sib, kinds], rc.at[kinds], core_send.at[g], core_recv.at[g], sibling)

    def core_arrival(g):
        kinds = kinds_of(g)
        return copy(rc.at[kinds], rc.at[kinds], core_send.at[g], core_recv.at[g], sibling)

    def take_o(q):
        copy(ho.at[q], ho.at[q], h_send.at[2 * q + c, 2], ho_recv.at[q], sibling).wait_recv()
        for p in range(SLABS):
            operand(0, c, p, hs[2 * q + c, p])
            operand(0, sib, p, ho[q, p])

    def take_y_x(q):
        k = 2 * q + c
        for core in range(2):
            copy(hy.at[q, core], hy.at[q, core], h_send.at[k, 0], hy_recv.at[q, core], sibling).wait_recv()
            copy(hx.at[q, core], hx.at[q, core], h_send.at[k, 1], hx_recv.at[q, core], sibling).wait_recv()
        for p in range(SLABS):
            for core in range(2):
                operand(1, core, p, hy[q, core, p])
                operand(2, core, p, hx[q, core, p])

    def products_y_x(q):
        product(1)
        product(2)
        pl.when(xl == q)(lambda: product(3))

    def products_w(q):
        @pl.when(w_half(y, c) == q)
        def _():
            for p in range(SLABS):
                for core in range(2):
                    piece = hw.at[core, p]
                    copy(piece, piece, wr_send.at[core, p], hw_recv.at[core, p], sibling).wait_recv()
                    operand(3, core, p, hw[core, p])
            product(4)
            if q == 1:
                core_copy(3).start()
            product(5)
            if q == 1:
                core_copy(4).start()

        if q == 1:

            @pl.when(w_half(y, c) != q)
            def _():
                core_copy(3).start()
                core_copy(4).start()

    mine = jnp.where(xh == y // 2, 0, 1)

    def up_copy(s, g):
        src = rc.at[kinds_of(g), (z + 4 - s) % 8]
        return copy(src, rp.at[s, kinds_of(g)], p_send.at[s, g], p_recv.at[s, g], z_up)

    def down_copy(s, g):
        src = rc.at[kinds_of(g), (z + 5 + s) % 8]
        return copy(src, rm.at[s, kinds_of(g)], m_send.at[s, g], m_recv.at[s, g], z_down)

    def sum_step(s, g):
        kinds = kinds_of(g)
        if s == 0:
            core_arrival(g).wait_recv()

            def add(d, _):
                rc[kinds, d] = rc[kinds, d] + kp[c, kinds, d]
                return 0

            lax.fori_loop(0, 8, add, 0)
        else:
            up_copy(s - 1, g).wait_recv()
            d = (z + 4 - s) % 8
            rc[kinds, d] = rc[kinds, d] + rp[s - 1, kinds]
            if s < 4:
                down_copy(s - 1, g).wait_recv()
                d = (z + 5 + s) % 8
                rc[kinds, d] = rc[kinds, d] + rm[s - 1, kinds]
        if s < 4:
            up_copy(s, g).start()
        if s < 3:
            down_copy(s, g).start()

    def level_copy(t):
        src = rc.at[2 * t + 1 - mine, z]
        return copy(src, re.at[t], e_send.at[t], e_recv.at[t], ((1 - xh) * 8 + z, r))

    def strip_copies(n):
        i_y = y + (mine, 1 - mine, 2, 2)[n]
        i_x = (xl + mine) % 2 if n == 1 else xl
        j_x = ((xl + mine) % 2, xl, xl, 1 - xl)[n]
        at_i = row_of(i_y, i_x, z // 4)
        at_j = row_of(y, j_x, c)
        slot = 0 if n < 2 else xh
        src = fp.at[n] if n < 2 else rc.at[n + 2, z]
        straight = ((at_i, at_j), rd.at[slot, z % 4], f_recv.at[0])
        turned = ((at_j, at_i), rt.at[slot, z % 4], f_recv.at[1])
        return src, straight, turned

    def each_strip(n, local, remote):
        src, *targets = strip_copies(n)
        for which, (to, dst, recv) in enumerate(targets):
            own = jnp.logical_and(to[0] == a, to[1] == r)
            wanted = jnp.logical_or(mine == 1, which == 0) if n == 0 else True

            if local is not None:

                @pl.when(jnp.logical_and(wanted, own))
                def _(dst=dst, recv=recv):
                    local(pltpu.make_async_copy(src, dst, recv))

            @pl.when(jnp.logical_and(wanted, jnp.logical_not(own)))
            def _(dst=dst, recv=recv, to=to, which=which):
                remote(copy(src, dst, f_send.at[n, which], recv, to))

    def hand_out(n):
        if n < 2:
            level_copy(n).wait_recv()
            fp[n] = rc[2 * n + mine, z] + re[n]
        each_strip(n, lambda one: one.start(), lambda one: one.start())

    def handed_out(n):
        each_strip(n, None, lambda one: one.wait_send())

    take_o(0)
    product(0)
    take_y_x(0)
    products_y_x(0)
    relay(2)
    products_w(0)
    relay(3, (0,))
    take_o(1)
    product(0)
    core_copy(0).start()
    relay(3, (1, 2))
    take_y_x(1)
    product(1)
    core_copy(1).start()
    product(2)
    pl.when(xl == 1)(lambda: product(3))
    core_copy(2).start()
    sum_step(0, 0)
    sum_step(0, 1)
    sum_step(1, 0)
    sum_step(0, 2)
    products_w(1)
    sum_step(1, 1)
    sum_step(2, 0)
    sum_step(1, 2)
    sum_step(0, 3)
    sum_step(2, 1)
    sum_step(0, 4)
    sum_step(3, 0)
    sum_step(2, 2)
    sum_step(1, 3)
    sum_step(3, 1)
    sum_step(1, 4)
    sum_step(4, 0)
    sum_step(3, 2)
    sum_step(2, 3)
    sum_step(4, 1)
    level_copy(0).start()
    sum_step(2, 4)
    sum_step(4, 2)
    level_copy(1).start()
    sum_step(3, 3)
    sum_step(3, 4)
    hand_out(0)
    sum_step(4, 3)
    hand_out(2)
    sum_step(4, 4)
    hand_out(3)
    hand_out(1)

    def sent(k, _):
        to_1, to_2, to_3 = h_copies(k)
        to_1.wait_send()
        to_2.wait_send()
        pl.when(k % 2 != c)(to_3.wait_send)
        for p in range(SLABS):
            pl.when(sends_w(k))(w_copy(k, p).wait_send)
            pl.when(relays(k))(relay_copy(k, p).wait_send)
        return 0

    def sent_plane(k, _):
        for j in range(3):
            to_y(k, j).wait_send()
        for j in range(4):
            for part in range(2):
                to_x(k, j, here, part).wait_send()
        for j in range(8):
            to_sibling(k, j, here, c).wait_send()
        return 0

    def sent_z(k, _):
        for s in range(4):
            to_far(k, s).wait_send()
        for s in range(3):
            to_near(k, s).wait_send()
        for j in range(8):
            z_sibling(k, c, j).wait_send()
        return 0

    lax.fori_loop(0, CHUNKS, sent, 0)
    lax.fori_loop(0, PLANE, sent_plane, 0)
    lax.fori_loop(PLANE, CHUNKS, sent_z, 0)
    for j in range(7):
        slices(j, here).wait_send()
    for g in range(5):
        core_copy(g).wait_send()
        for s in range(4):
            up_copy(s, g).wait_send()
        for s in range(3):
            down_copy(s, g).wait_send()

    for t in range(2):
        level_copy(t).wait_send()

    apart = (y - a // 4 + 4) % 4
    across_x = xl != (a // 2) % 2

    def gather(strips, sem, block):
        @pl.when(apart == 2)
        def _():
            pltpu.make_async_copy(strips, strips, sem).wait()
            strips[0] = strips[0] + strips[1]

        @pl.when(apart != 2)
        def _():
            pltpu.make_async_copy(strips.at[0], strips.at[0], sem).wait()

        for n in range(4):
            rest = strips[0, n, STRIP:PACK]
            at = n * STRIP
            block[at : at + STRIP, 0:LANES] = strips[0, n, 0:STRIP]
            block[at : at + STRIP // 2, LANES:ROWS] = rest[:, 0 : ROWS - LANES]
            block[at + STRIP // 2 : at + STRIP, LANES:ROWS] = rest[:, ROWS - LANES : LANES]

    @pl.when(apart != 1)
    def _():
        gather(rd, f_recv.at[0], out)

    @pl.when(apart == 1)
    def _():
        out[...] = jnp.zeros_like(out)

    @pl.when(jnp.logical_and(apart != 3, jnp.logical_or(apart != 0, across_x)))
    def _():
        gather(rt, f_recv.at[1], ft)
        out[...] = out[...] + ft[...].T

    for n in range(4):
        handed_out(n)


def per_device(factors, orbitals, tile_mask):
    dma = pltpu.SemaphoreType.DMA
    vmem = pltpu.VMEM
    part = (SLABS, ROWS, LANES)
    return pl.pallas_call(
        kernel,
        out_shape=jax.ShapeDtypeStruct((ROWS, ROWS), F32),
        in_specs=[
            pl.BlockSpec(memory_space=pl.ANY),
            pl.BlockSpec(memory_space=pltpu.VMEM),
            pl.BlockSpec(memory_space=pltpu.SMEM),
        ],
        out_specs=pl.BlockSpec(memory_space=pltpu.VMEM),
        scratch_shapes=[
            vmem((SLABS, ROWS, 3072), F32),
            vmem((SLABS, ROWS, 3072), BF16),
            vmem((SLABS, ROWS, 3072), BF16),
            vmem((CHUNKS, 2, 8, ROWS, LANES), F32),
            vmem((3072, 2 * LANES), BF16),
            vmem((CHUNKS, *part), F32),
            vmem((2, *part), F32),
            vmem((2, 2, *part), F32),
            vmem((2, 2, *part), F32),
            vmem((2, *part), F32),
            vmem((2, *part), F32),
            vmem((4, PAIR, 3 * SLABS * LANES), BF16),
            vmem((2, PAIR, 3 * SLABS * LANES), BF16),
            vmem((2, 6, 8, PACK, LANES), F32),
            vmem((6, 8, PACK, LANES), F32),
            vmem((4, 6, PACK, LANES), F32),
            vmem((3, 6, PACK, LANES), F32),
            vmem((2, PACK, LANES), F32),
            vmem((2, PACK, LANES), F32),
            vmem((2, 4, PACK, LANES), F32),
            vmem((2, 4, PACK, LANES), F32),
            vmem((ROWS, ROWS), F32),
            dma((SLABS,)),
            dma((CHUNKS, 3)), dma((CHUNKS, 3)),
            dma((CHUNKS, 4, 2)), dma((CHUNKS, 4, 2)),
            dma((CHUNKS, 8)), dma((CHUNKS, 8)),
            dma((7,)), dma((7,)), dma((CHUNKS, 4)), dma((CHUNKS, 4)), dma((CHUNKS, 3)), dma((CHUNKS, 3)),
            dma((CHUNKS, 8)), dma((CHUNKS, 8)),
            dma((CHUNKS, 3)), dma((CHUNKS, SLABS)), dma((2,)), dma((2, 2)), dma((2, 2)),
            dma((2, SLABS)), dma((2, SLABS)), dma((2, SLABS)),
            dma((5,)), dma((5,)),
            dma((4, 5)), dma((4, 5)), dma((3, 5)), dma((3, 5)),
            dma((2,)), dma((2,)),
            dma((4, 2)), dma((2,)),
        ],
        compiler_params=pltpu.CompilerParams(
            collective_id=0, has_side_effects=True, vmem_limit_bytes=60 * 2**20
        ),
    )(factors, orbitals, tile_mask)


def solution(mesh):
    placed = (P("aux", "row", None), P("row", None), P("aux", None, None))
    return jax.shard_map(
        per_device, mesh=mesh, in_specs=placed, out_specs=P("aux", "row"), check_vma=False
    )
```

```python
import jax
import jax.numpy as jnp
from jax import lax
from jax.experimental import pallas as pl
from jax.experimental.pallas import tpu as pltpu
from jax.sharding import PartitionSpec as P

F32 = jnp.float32
BF16 = jnp.bfloat16
MESH = pl.DeviceIdType.MESH
ROWS = 192
PAIR = 384
LANES = 128
CHUNKS = 4
PLANE = 2
SLICE = 24
SLABS = 3
STRIP = 48
PACK = 72
STEPS_Y = (1, -1, 2)


def split(value):
    high = value.astype(BF16)
    return high, (value - high.astype(F32)).astype(BF16)


def kernel(
    b_hbm, c_ref, mask, out,
    bf, bh, bl, cb, ch, hs, ho, hy, hx, hw, wr, left, right, kp, rc, rp, rm, re, fp, rd, rt, ft,
    sem_b, y_send, y_recv, x_send, x_recv, s_send, s_recv,
    g_send, g_recv, long_send, long_recv, short_send, short_recv, zs_send, zs_recv,
    h_send, w_send, ho_recv, hy_recv, hx_recv, hw_recv, wr_send, wr_recv,
    core_send, core_recv, p_send, p_recv, m_send, m_recv, e_send, e_recv, f_send, f_recv,
):
    a, r = lax.axis_index("aux"), lax.axis_index("row")
    xh, z = a // 8, a % 8
    y, xl, c = r // 4, (r // 2) % 2, r % 2
    sib = 1 - c

    def row_of(yy, xx, cc):
        return ((yy + 4) % 4 * 2 + xx) * 2 + cc

    def dev(yy, xx, cc):
        return (a, row_of(yy, xx, cc))

    def copy(src, dst, send, recv, to):
        return pltpu.make_async_remote_copy(
            src_ref=src, dst_ref=dst, send_sem=send, recv_sem=recv, device_id=to, device_id_type=MESH
        )

    across = ((a, row_of(y, 1 - xl, c)), ((1 - xh) * 8 + z, row_of(y, 1 - xl, c)))
    sibling = dev(y, xl, sib)
    z_up = (xh * 8 + (z + 1) % 8, r)
    z_down = (xh * 8 + (z + 7) % 8, r)

    slab_copies = [pltpu.make_async_copy(b_hbm.at[p], bf.at[p], sem_b.at[p]) for p in range(SLABS)]
    for each in slab_copies:
        each.start()

    here = 2 * y + xl
    for k in range(CHUNKS):
        cb[k, c, here] = c_ref[:, k * LANES : (k + 1) * LANES]

    barrier = pltpu.get_barrier_semaphore()
    peers = [dev(y + dy, xl, c) for dy in STEPS_Y] + [dev(y + dy, 1 - xl, c) for dy in (0, *STEPS_Y)]
    greeted = [
        *peers, across[1], sibling, z_up, z_down,
    ]
    for each in greeted:
        pl.semaphore_signal(barrier, inc=1, device_id=each, device_id_type=MESH)
    pl.semaphore_wait(barrier, len(greeted))

    def place(yy, xx):
        return (yy + 4) % 4 * 2 + xx

    def to_y(k, j):
        block = cb.at[k, c, here]
        return copy(block, block, y_send.at[k, j], y_recv.at[k, j], dev(y + STEPS_Y[j], xl, c))

    def from_y(k, j):
        block = cb.at[k, c, place(y - STEPS_Y[j], xl)]
        return copy(block, block, y_send.at[k, j], y_recv.at[k, j], sibling)

    def to_x(k, j, at, part):
        piece = cb.at[k, c, at, pl.ds(96 * part, 96)]
        return copy(piece, piece, x_send.at[k, j, part], x_recv.at[k, j, part], across[part])

    def to_sibling(k, j, at, core):
        block = cb.at[k, core, at]
        return copy(block, block, s_send.at[k, j], s_recv.at[k, j], sibling)

    def y_place(j, xx):
        return place(y - STEPS_Y[j], xx) if j < 3 else place(y, xx)

    def first(k):
        for j in range(3):
            to_y(k, j).start()
        for part in range(2):
            to_x(k, 3, here, part).start()
        to_sibling(k, 3, here, c).start()

    def forward_y(k):
        for j in range(3):
            from_y(k, j).wait_recv()
            at = y_place(j, xl)
            for part in range(2):
                to_x(k, j, at, part).start()
            to_sibling(k, j, at, c).start()

    def forward_x(k):
        for j in (3, 0, 1, 2):
            at = y_place(j, 1 - xl)
            for part in range(2):
                to_x(k, j, at, part).wait_recv()
            to_sibling(k, 4 + j, at, c).start()

    def slices(j, at):
        piece = cb.at[pl.ds(PLANE, CHUNKS - PLANE), c, at, pl.ds(SLICE * z, SLICE)]
        return copy(piece, piece, g_send.at[j], g_recv.at[j], peers[j])

    far = 1 - 2 * c
    z_far = (xh * 8 + (z + 8 + far) % 8, r)
    z_near = (xh * 8 + (z + 8 - far) % 8, r)

    def z_piece(k, core, at):
        return cb.at[k, core, :, pl.ds(SLICE * ((z + 8 + at) % 8), SLICE)]

    def to_far(k, s):
        piece = z_piece(k, c, -far * s)
        return copy(piece, piece, long_send.at[k, s], long_recv.at[k, s], z_far)

    def from_far(k, s):
        piece = z_piece(k, c, -far * (s + 1))
        return copy(piece, piece, long_send.at[k, s], long_recv.at[k, s], z_far)

    def to_near(k, s):
        piece = z_piece(k, c, far * s)
        return copy(piece, piece, short_send.at[k, s], short_recv.at[k, s], z_near)

    def from_near(k, s):
        piece = z_piece(k, c, far * (s + 1))
        return copy(piece, piece, short_send.at[k, s], short_recv.at[k, s], z_near)

    def z_sibling(k, core, j):
        piece = z_piece(k, core, j)
        at = (j + 8) % 8
        return copy(piece, piece, zs_send.at[k, at], zs_recv.at[k, at], sibling)

    def plane_slices():
        for j in range(7):
            slices(j, here).start()

    def z_first():
        for j in range(7):
            at = place(y - STEPS_Y[j], xl) if j < 3 else place(y, 1 - xl) if j == 3 else place(y - STEPS_Y[j - 4], 1 - xl)
            slices(j, at).wait_recv()

    def z_own(k):
        to_far(k, 0).start()
        to_near(k, 0).start()
        z_sibling(k, c, 0).start()

    def z_step(k, s):
        from_far(k, s).wait_recv()
        if s < 3:
            to_far(k, s + 1).start()
        z_sibling(k, c, -far * (s + 1)).start()
        if s < 3:
            from_near(k, s).wait_recv()
            if s < 2:
                to_near(k, s + 1).start()
            z_sibling(k, c, far * (s + 1)).start()

    def whole(k):
        if k < PLANE:
            for j in range(4):
                to_sibling(k, j, y_place(j, xl), sib).wait_recv()
                to_sibling(k, 4 + j, y_place(j, 1 - xl), sib).wait_recv()
        else:
            for j in range(8):
                z_sibling(k, sib, j).wait_recv()

    def screen(p):
        slab_copies[p].wait()

        def tile(n, _):
            at = pl.ds(pl.multiple_of(n * LANES, LANES), LANES)
            for g in range(3):
                keep = mask[p, (3 * r + g) // 2, n].astype(F32)
                rows = pl.ds(64 * g, 64)
                high, low = split(bf[p, rows, at] * keep)
                bh[p, rows, at] = high
                bl[p, rows, at] = low
            return 0

        lax.fori_loop(0, 24, tile, 0, unroll=4)

    def half(k):
        def block(n, _):
            high, low = split(cb[k, n % 2, n // 2])
            at = pl.ds(pl.multiple_of(n * ROWS, ROWS), ROWS)
            ch[at, 0:LANES] = high
            ch[at, LANES : 2 * LANES] = low
            return 0

        lax.fori_loop(0, 16, block, 0)

        for p in range(SLABS):
            both = jnp.dot(bh[p], ch[...], preferred_element_type=F32)
            low = jnp.dot(bl[p], ch[:, 0:LANES], preferred_element_type=F32)
            hs[k, p] = both[:, 0:LANES] + (both[:, LANES : 2 * LANES] + low)
            send_half(k, p)

    def h_copies(k, p=slice(None)):
        h, q = k % 2, k // 2
        src = hs.at[k, p]
        return (
            copy(src, hy.at[q, c, p], h_send.at[k, 0], hy_recv.at[q, c], dev(y - 1, xl, h)),
            copy(src, hx.at[q, c, p], h_send.at[k, 1], hx_recv.at[q, c], dev(y, 1 - xl, h)),
            copy(src, ho.at[q, p], h_send.at[k, 2], ho_recv.at[q], sibling),
        )

    def w_copy(k, p):
        h = k % 2
        return copy(hs.at[k, p], wr.at[h, p], w_send.at[k, p], wr_recv.at[h, p], dev(y + 1, xl, c))

    def w_half(yy, core):
        return ((yy + 4) % 4 // 2 + core) % 2

    def sends_w(k):
        return k // 2 == w_half(y + 2, k % 2)

    def send_half(k, p):
        pl.when(sends_w(k))(w_copy(k, p).start)
        to_1, to_2, to_3 = h_copies(k, p)
        to_1.start()
        to_2.start()
        pl.when(k % 2 != c)(to_3.start)

    def relay_copy(k, p):
        h = k % 2
        return copy(wr.at[h, p], hw.at[c, p], wr_send.at[h, p], hw_recv.at[c, p], dev(y + 1, xl, h))

    def relays(k):
        return k // 2 == w_half(y + 1, k % 2)

    def relay(k, slabs=range(SLABS)):
        @pl.when(relays(k))
        def _():
            h = k % 2
            for p in slabs:
                copy(wr.at[h, p], wr.at[h, p], wr_send.at[h, p], wr_recv.at[h, p], sibling).wait_recv()
                relay_copy(k, p).start()

    plane_slices()
    first(0)
    kp[...] = jnp.zeros_like(kp)
    screen(0)
    z_first()
    z_own(2)
    z_own(3)
    forward_y(0)
    first(1)
    screen(1)
    z_step(2, 0)
    z_step(3, 0)
    forward_x(0)
    forward_y(1)
    screen(2)
    z_step(2, 1)
    whole(0)
    half(0)
    forward_x(1)
    z_step(3, 1)
    z_step(2, 2)
    whole(1)
    half(1)
    z_step(3, 2)
    z_step(2, 3)
    whole(2)
    half(2)
    z_step(3, 3)
    relay(0)
    relay(1)
    whole(3)
    half(3)

    def operand(slot, core, p, value):
        rows = pl.ds(pl.multiple_of(core * ROWS, ROWS), ROWS)
        high, low = split(value)
        for where, part in ((0, high), (1, low), (2, high)):
            left[slot, rows, pl.ds((where * SLABS + p) * LANES, LANES)] = part
        if slot in (0, 2):
            for where, part in ((0, high), (1, high), (2, low)):
                right[slot // 2, rows, pl.ds((where * SLABS + p) * LANES, LANES)] = part

    def product(kind):
        rows, columns = ((0, 0), (1, 1), (1, 0), (2, 0), (3, 0), (3, 1))[kind]

        def one(core, _):
            at = pl.ds(pl.multiple_of(core * ROWS, ROWS), ROWS)
            value = lax.dot_general(
                left[rows], right[columns, at], (((1,), (1,)), ((), ())), preferred_element_type=F32
            )
            rest = value[:, LANES:ROWS].reshape(8, 2, STRIP // 2, ROWS - LANES)
            rest = jnp.concatenate([rest[:, 0], rest[:, 1]], axis=-1)
            kp[core, kind, :, 0:STRIP] += value[:, 0:LANES].reshape(8, STRIP, LANES)
            kp[core, kind, :, STRIP:PACK] += rest
            return 0

        lax.fori_loop(0, 2, one, 0)

    def kinds_of(g):
        start, count = ((0, 1), (1, 1), (2, 2), (4, 1), (5, 1))[g]
        return pl.ds(start, count)

    def core_copy(g):
        kinds = kinds_of(g)
        return copy(kp.at[sib, kinds], rc.at[kinds], core_send.at[g], core_recv.at[g], sibling)

    def core_arrival(g):
        kinds = kinds_of(g)
        return copy(rc.at[kinds], rc.at[kinds], core_send.at[g], core_recv.at[g], sibling)

    def take_o(q):
        copy(ho.at[q], ho.at[q], h_send.at[2 * q + c, 2], ho_recv.at[q], sibling).wait_recv()
        for p in range(SLABS):
            operand(0, c, p, hs[2 * q + c, p])
            operand(0, sib, p, ho[q, p])

    def take_y_x(q):
        k = 2 * q + c
        for core in range(2):
            copy(hy.at[q, core], hy.at[q, core], h_send.at[k, 0], hy_recv.at[q, core], sibling).wait_recv()
            copy(hx.at[q, core], hx.at[q, core], h_send.at[k, 1], hx_recv.at[q, core], sibling).wait_recv()
        for p in range(SLABS):
            for core in range(2):
                operand(1, core, p, hy[q, core, p])
                operand(2, core, p, hx[q, core, p])

    def products_y_x(q):
        product(1)
        product(2)
        pl.when(xl == q)(lambda: product(3))

    def products_w(q):
        @pl.when(w_half(y, c) == q)
        def _():
            for p in range(SLABS):
                for core in range(2):
                    piece = hw.at[core, p]
                    copy(piece, piece, wr_send.at[core, p], hw_recv.at[core, p], sibling).wait_recv()
                    operand(3, core, p, hw[core, p])
            product(4)
            if q == 1:
                core_copy(3).start()
            product(5)
            if q == 1:
                core_copy(4).start()

        if q == 1:

            @pl.when(w_half(y, c) != q)
            def _():
                core_copy(3).start()
                core_copy(4).start()

    mine = jnp.where(xh == y // 2, 0, 1)

    def far_slice(s):
        return (z + 8 + far * (4 - s)) % 8

    def near_slice(s):
        return (z + 8 - far * (3 - s)) % 8

    def far_copy(s, g):
        src = rc.at[kinds_of(g), far_slice(s)]
        return copy(src, rp.at[s, kinds_of(g)], p_send.at[s, g], p_recv.at[s, g], z_far)

    def near_copy(s, g):
        src = rc.at[kinds_of(g), near_slice(s)]
        return copy(src, rm.at[s, kinds_of(g)], m_send.at[s, g], m_recv.at[s, g], z_near)

    def sum_step(s, g):
        kinds = kinds_of(g)
        if s == 0:
            core_arrival(g).wait_recv()

            def add(d, _):
                rc[kinds, d] = rc[kinds, d] + kp[c, kinds, d]
                return 0

            lax.fori_loop(0, 8, add, 0)
        else:
            far_copy(s - 1, g).wait_recv()
            d = far_slice(s)
            rc[kinds, d] = rc[kinds, d] + rp[s - 1, kinds]
            if s < 4:
                near_copy(s - 1, g).wait_recv()
                d = near_slice(s)
                rc[kinds, d] = rc[kinds, d] + rm[s - 1, kinds]
        if s < 4:
            far_copy(s, g).start()
        if s < 3:
            near_copy(s, g).start()

    def level_copy(t):
        src = rc.at[2 * t + 1 - mine, z]
        return copy(src, re.at[t], e_send.at[t], e_recv.at[t], ((1 - xh) * 8 + z, r))

    def strip_copies(n):
        i_y = y + (mine, 1 - mine, 2)[n]
        i_x = (xl + mine) % 2 if n == 1 else xl
        j_x = xl if n == 1 else (xl + mine) % 2
        at_i = row_of(i_y, i_x, z // 4)
        at_j = row_of(y, j_x, c)
        straight = ((at_i, at_j), rd.at[z % 4], f_recv.at[0])
        turned = ((at_j, at_i), rt.at[z % 4], f_recv.at[1])
        return fp.at[n], straight, turned

    def each_strip(n, local, remote):
        src, *targets = strip_copies(n)
        for which, (to, dst, recv) in enumerate(targets):
            own = jnp.logical_and(to[0] == a, to[1] == r)
            wanted = jnp.logical_or(mine == 1, which == 0) if n == 0 else True

            if local is not None:

                @pl.when(jnp.logical_and(wanted, own))
                def _(dst=dst, recv=recv):
                    local(pltpu.make_async_copy(src, dst, recv))

            @pl.when(jnp.logical_and(wanted, jnp.logical_not(own)))
            def _(dst=dst, recv=recv, to=to, which=which):
                remote(copy(src, dst, f_send.at[n, which], recv, to))

    def hand_out(n):
        level_copy(n).wait_recv()
        fp[n] = rc[2 * n + mine, z] + re[n]
        each_strip(n, lambda one: one.start(), lambda one: one.start())

    def handed_out(n):
        each_strip(n, None, lambda one: one.wait_send())

    take_o(0)
    product(0)
    take_y_x(0)
    relay(2)
    products_y_x(0)
    relay(3, (0,))
    products_w(0)
    relay(3, (1, 2))
    take_o(1)
    product(0)
    core_copy(0).start()
    take_y_x(1)
    product(1)
    core_copy(1).start()
    product(2)
    pl.when(xl == 1)(lambda: product(3))
    core_copy(2).start()
    sum_step(0, 0)
    sum_step(0, 1)
    sum_step(1, 0)
    sum_step(0, 2)
    products_w(1)
    sum_step(1, 1)
    sum_step(0, 3)
    sum_step(0, 4)
    sum_step(2, 0)
    sum_step(1, 2)
    sum_step(2, 1)
    sum_step(1, 3)
    sum_step(1, 4)
    sum_step(3, 0)
    sum_step(2, 2)
    sum_step(3, 1)
    sum_step(2, 3)
    sum_step(2, 4)
    sum_step(4, 0)
    sum_step(3, 2)
    sum_step(4, 1)
    level_copy(0).start()
    sum_step(3, 3)
    sum_step(3, 4)
    sum_step(4, 2)
    level_copy(1).start()
    sum_step(4, 3)
    sum_step(4, 4)
    level_copy(2).start()
    hand_out(0)
    hand_out(1)
    hand_out(2)

    def sent(k, _):
        to_1, to_2, to_3 = h_copies(k)
        to_1.wait_send()
        to_2.wait_send()
        pl.when(k % 2 != c)(to_3.wait_send)
        for p in range(SLABS):
            pl.when(sends_w(k))(w_copy(k, p).wait_send)
            pl.when(relays(k))(relay_copy(k, p).wait_send)
        return 0

    def sent_plane(k, _):
        for j in range(3):
            to_y(k, j).wait_send()
        for j in range(4):
            for part in range(2):
                to_x(k, j, here, part).wait_send()
        for j in range(8):
            to_sibling(k, j, here, c).wait_send()
        return 0

    def sent_z(k, _):
        for s in range(4):
            to_far(k, s).wait_send()
        for s in range(3):
            to_near(k, s).wait_send()
        for j in range(8):
            z_sibling(k, c, j).wait_send()
        return 0

    lax.fori_loop(0, CHUNKS, sent, 0)
    lax.fori_loop(0, PLANE, sent_plane, 0)
    lax.fori_loop(PLANE, CHUNKS, sent_z, 0)
    for j in range(7):
        slices(j, here).wait_send()
    for g in range(5):
        core_copy(g).wait_send()
        for s in range(4):
            far_copy(s, g).wait_send()
        for s in range(3):
            near_copy(s, g).wait_send()

    for t in range(3):
        level_copy(t).wait_send()

    apart = (y - a // 4 + 4) % 4
    across_x = xl != (a // 2) % 2

    def gather(strips, sem, block):
        pltpu.make_async_copy(strips, strips, sem).wait()
        for n in range(4):
            rest = strips[n, STRIP:PACK]
            at = n * STRIP
            block[at : at + STRIP, 0:LANES] = strips[n, 0:STRIP]
            block[at : at + STRIP // 2, LANES:ROWS] = rest[:, 0 : ROWS - LANES]
            block[at + STRIP // 2 : at + STRIP, LANES:ROWS] = rest[:, ROWS - LANES : LANES]

    @pl.when(apart != 1)
    def _():
        gather(rd, f_recv.at[0], out)

    @pl.when(apart == 1)
    def _():
        out[...] = jnp.zeros_like(out)

    @pl.when(jnp.logical_and(apart != 3, jnp.logical_or(apart != 0, across_x)))
    def _():
        gather(rt, f_recv.at[1], ft)
        out[...] = out[...] + ft[...].T

    for n in range(3):
        handed_out(n)


def per_device(factors, orbitals, tile_mask):
    dma = pltpu.SemaphoreType.DMA
    vmem = pltpu.VMEM
    part = (SLABS, ROWS, LANES)
    return pl.pallas_call(
        kernel,
        out_shape=jax.ShapeDtypeStruct((ROWS, ROWS), F32),
        in_specs=[
            pl.BlockSpec(memory_space=pl.ANY),
            pl.BlockSpec(memory_space=pltpu.VMEM),
            pl.BlockSpec(memory_space=pltpu.SMEM),
        ],
        out_specs=pl.BlockSpec(memory_space=pltpu.VMEM),
        scratch_shapes=[
            vmem((SLABS, ROWS, 3072), F32),
            vmem((SLABS, ROWS, 3072), BF16),
            vmem((SLABS, ROWS, 3072), BF16),
            vmem((CHUNKS, 2, 8, ROWS, LANES), F32),
            vmem((3072, 2 * LANES), BF16),
            vmem((CHUNKS, *part), F32),
            vmem((2, *part), F32),
            vmem((2, 2, *part), F32),
            vmem((2, 2, *part), F32),
            vmem((2, *part), F32),
            vmem((2, *part), F32),
            vmem((4, PAIR, 3 * SLABS * LANES), BF16),
            vmem((2, PAIR, 3 * SLABS * LANES), BF16),
            vmem((2, 6, 8, PACK, LANES), F32),
            vmem((6, 8, PACK, LANES), F32),
            vmem((4, 6, PACK, LANES), F32),
            vmem((3, 6, PACK, LANES), F32),
            vmem((3, PACK, LANES), F32),
            vmem((3, PACK, LANES), F32),
            vmem((4, PACK, LANES), F32),
            vmem((4, PACK, LANES), F32),
            vmem((ROWS, ROWS), F32),
            dma((SLABS,)),
            dma((CHUNKS, 3)), dma((CHUNKS, 3)),
            dma((CHUNKS, 4, 2)), dma((CHUNKS, 4, 2)),
            dma((CHUNKS, 8)), dma((CHUNKS, 8)),
            dma((7,)), dma((7,)), dma((CHUNKS, 4)), dma((CHUNKS, 4)), dma((CHUNKS, 3)), dma((CHUNKS, 3)),
            dma((CHUNKS, 8)), dma((CHUNKS, 8)),
            dma((CHUNKS, 3)), dma((CHUNKS, SLABS)), dma((2,)), dma((2, 2)), dma((2, 2)),
            dma((2, SLABS)), dma((2, SLABS)), dma((2, SLABS)),
            dma((5,)), dma((5,)),
            dma((4, 5)), dma((4, 5)), dma((3, 5)), dma((3, 5)),
            dma((3,)), dma((3,)),
            dma((3, 2)), dma((2,)),
        ],
        compiler_params=pltpu.CompilerParams(
            collective_id=0, has_side_effects=True, vmem_limit_bytes=60 * 2**20
        ),
    )(factors, orbitals, tile_mask)


def solution(mesh):
    placed = (P("aux", "row", None), P("row", None), P("aux", None, None))
    return jax.shard_map(
        per_device, mesh=mesh, in_specs=placed, out_specs=P("aux", "row"), check_vma=False
    )
```

```python
import functools

import jax
import jax.numpy as jnp
from jax import lax
from jax.experimental import pallas as pl
from jax.experimental.pallas import tpu as pltpu
from jax.sharding import PartitionSpec as P

F32 = jnp.float32
BF16 = jnp.bfloat16
MESH = pl.DeviceIdType.MESH
ROWS = 192
PAIR = 384
LANES = 128
CHUNKS = 4
PLANE = 2
SLICE = 24
SLABS = 3
STRIP = 48
PACK = 72
STEPS_Y = (1, -1, 2)


def split(value):
    high = value.astype(BF16)
    return high, (value - high.astype(F32)).astype(BF16)


def kernel(
    b_hbm, c_ref, mask, out,
    bf, bh, bl, cb, ch, hs, ho, hy, hx, hw, wr, left, right, kp, rc, rp, rm, fin, fp, rd, rt, ft,
    sem_b, y_send, y_recv, x_send, x_recv, s_send, s_recv,
    g_send, g_recv, long_send, long_recv, short_send, short_recv, zs_send, zs_recv,
    h_send, w_send, ho_recv, hy_recv, hx_recv, hw_recv, wr_send, wr_recv,
    core_send, core_recv, p_send, p_recv, m_send, m_recv, l_send, l_recv, f_send, f_recv,
):
    a, r = lax.axis_index("aux"), lax.axis_index("row")
    xh, z = a // 8, a % 8
    y, xl, c = r // 4, (r // 2) % 2, r % 2
    sib = 1 - c

    def row_of(yy, xx, cc):
        return ((yy + 4) % 4 * 2 + xx) * 2 + cc

    def dev(yy, xx, cc):
        return (a, row_of(yy, xx, cc))

    def copy(src, dst, send, recv, to):
        return pltpu.make_async_remote_copy(
            src_ref=src, dst_ref=dst, send_sem=send, recv_sem=recv, device_id=to, device_id_type=MESH
        )

    across = ((a, row_of(y, 1 - xl, c)), ((1 - xh) * 8 + z, row_of(y, 1 - xl, c)))
    sibling = dev(y, xl, sib)
    z_up = (xh * 8 + (z + 1) % 8, r)
    z_down = (xh * 8 + (z + 7) % 8, r)

    slab_copies = [pltpu.make_async_copy(b_hbm.at[p], bf.at[p], sem_b.at[p]) for p in range(SLABS)]
    for each in slab_copies:
        each.start()

    here = 2 * y + xl
    for k in range(CHUNKS):
        cb[k, c, here] = c_ref[:, k * LANES : (k + 1) * LANES]

    barrier = pltpu.get_barrier_semaphore()
    peers = [dev(y + dy, xl, c) for dy in STEPS_Y] + [dev(y + dy, 1 - xl, c) for dy in (0, *STEPS_Y)]
    greeted = [
        *peers, across[1], sibling, z_up, z_down,
    ]
    for each in greeted:
        pl.semaphore_signal(barrier, inc=1, device_id=each, device_id_type=MESH)
    pl.semaphore_wait(barrier, len(greeted))

    def place(yy, xx):
        return (yy + 4) % 4 * 2 + xx

    def to_y(k, j):
        block = cb.at[k, c, here]
        return copy(block, block, y_send.at[k, j], y_recv.at[k, j], dev(y + STEPS_Y[j], xl, c))

    def from_y(k, j):
        block = cb.at[k, c, place(y - STEPS_Y[j], xl)]
        return copy(block, block, y_send.at[k, j], y_recv.at[k, j], sibling)

    def to_x(k, j, at, part):
        piece = cb.at[k, c, at, pl.ds(96 * part, 96)]
        return copy(piece, piece, x_send.at[k, j, part], x_recv.at[k, j, part], across[part])

    def to_sibling(k, j, at, core):
        block = cb.at[k, core, at]
        return copy(block, block, s_send.at[k, j], s_recv.at[k, j], sibling)

    def y_place(j, xx):
        return place(y - STEPS_Y[j], xx) if j < 3 else place(y, xx)

    def first(k):
        for j in range(3):
            to_y(k, j).start()
        for part in range(2):
            to_x(k, 3, here, part).start()
        to_sibling(k, 3, here, c).start()

    def forward_y(k):
        for j in range(3):
            from_y(k, j).wait_recv()
            at = y_place(j, xl)
            for part in range(2):
                to_x(k, j, at, part).start()
            to_sibling(k, j, at, c).start()

    def forward_x(k):
        for j in (3, 0, 1, 2):
            at = y_place(j, 1 - xl)
            for part in range(2):
                to_x(k, j, at, part).wait_recv()
            to_sibling(k, 4 + j, at, c).start()

    def slices(j, at):
        piece = cb.at[pl.ds(PLANE, CHUNKS - PLANE), c, at, pl.ds(SLICE * z, SLICE)]
        return copy(piece, piece, g_send.at[j], g_recv.at[j], peers[j])

    far = 1 - 2 * c
    z_far = (xh * 8 + (z + 8 + far) % 8, r)
    z_near = (xh * 8 + (z + 8 - far) % 8, r)

    def z_piece(k, core, at):
        return cb.at[k, core, :, pl.ds(SLICE * ((z + 8 + at) % 8), SLICE)]

    def to_far(k, s):
        piece = z_piece(k, c, -far * s)
        return copy(piece, piece, long_send.at[k, s], long_recv.at[k, s], z_far)

    def from_far(k, s):
        piece = z_piece(k, c, -far * (s + 1))
        return copy(piece, piece, long_send.at[k, s], long_recv.at[k, s], z_far)

    def to_near(k, s):
        piece = z_piece(k, c, far * s)
        return copy(piece, piece, short_send.at[k, s], short_recv.at[k, s], z_near)

    def from_near(k, s):
        piece = z_piece(k, c, far * (s + 1))
        return copy(piece, piece, short_send.at[k, s], short_recv.at[k, s], z_near)

    def z_sibling(k, core, j):
        piece = z_piece(k, core, j)
        at = (j + 8) % 8
        return copy(piece, piece, zs_send.at[k, at], zs_recv.at[k, at], sibling)

    def plane_slices():
        for j in range(7):
            slices(j, here).start()

    def z_first():
        for j in range(7):
            at = place(y - STEPS_Y[j], xl) if j < 3 else place(y, 1 - xl) if j == 3 else place(y - STEPS_Y[j - 4], 1 - xl)
            slices(j, at).wait_recv()

    def z_own(k):
        to_far(k, 0).start()
        to_near(k, 0).start()
        z_sibling(k, c, 0).start()

    def z_step(k, s):
        from_far(k, s).wait_recv()
        if s < 3:
            to_far(k, s + 1).start()
        z_sibling(k, c, -far * (s + 1)).start()
        if s < 3:
            from_near(k, s).wait_recv()
            if s < 2:
                to_near(k, s + 1).start()
            z_sibling(k, c, far * (s + 1)).start()

    def whole(k):
        if k < PLANE:
            for j in range(4):
                to_sibling(k, j, y_place(j, xl), sib).wait_recv()
                to_sibling(k, 4 + j, y_place(j, 1 - xl), sib).wait_recv()
        else:
            for j in range(8):
                z_sibling(k, sib, j).wait_recv()

    def screen(p):
        slab_copies[p].wait()

        def tile(n, _):
            at = pl.ds(pl.multiple_of(n * LANES, LANES), LANES)
            for g in range(3):
                keep = mask[p, (3 * r + g) // 2, n].astype(F32)
                rows = pl.ds(64 * g, 64)
                high, low = split(bf[p, rows, at] * keep)
                bh[p, rows, at] = high
                bl[p, rows, at] = low
            return 0

        lax.fori_loop(0, 24, tile, 0, unroll=4)

    def half(k):
        def block(n, _):
            high, low = split(cb[k, n % 2, n // 2])
            at = pl.ds(pl.multiple_of(n * ROWS, ROWS), ROWS)
            ch[at, 0:LANES] = high
            ch[at, LANES : 2 * LANES] = low
            return 0

        lax.fori_loop(0, 16, block, 0)

        for p in range(SLABS):
            both = jnp.dot(bh[p], ch[...], preferred_element_type=F32)
            low = jnp.dot(bl[p], ch[:, 0:LANES], preferred_element_type=F32)
            hs[k, p] = both[:, 0:LANES] + (both[:, LANES : 2 * LANES] + low)
            send_half(k, p)

    def h_copies(k, p=slice(None)):
        h, q = k % 2, k // 2
        src = hs.at[k, p]
        return (
            copy(src, hy.at[q, c, p], h_send.at[k, 0], hy_recv.at[q, c], dev(y - 1, xl, h)),
            copy(src, hx.at[q, c, p], h_send.at[k, 1], hx_recv.at[q, c], dev(y, 1 - xl, h)),
            copy(src, ho.at[q, p], h_send.at[k, 2], ho_recv.at[q], sibling),
        )

    def w_copy(k, p):
        h = k % 2
        return copy(hs.at[k, p], wr.at[h, p], w_send.at[k, p], wr_recv.at[h, p], dev(y + 1, xl, c))

    def w_half(yy, core):
        return ((yy + 4) % 4 // 2 + core) % 2

    def sends_w(k):
        return k // 2 == w_half(y + 2, k % 2)

    def send_half(k, p):
        pl.when(sends_w(k))(w_copy(k, p).start)
        to_1, to_2, to_3 = h_copies(k, p)
        to_1.start()
        to_2.start()
        pl.when(k % 2 != c)(to_3.start)

    def relay_copy(k, p):
        h = k % 2
        return copy(wr.at[h, p], hw.at[c, p], wr_send.at[h, p], hw_recv.at[c, p], dev(y + 1, xl, h))

    def relays(k):
        return k // 2 == w_half(y + 1, k % 2)

    def relay(k, slabs=range(SLABS)):
        @pl.when(relays(k))
        def _():
            h = k % 2
            for p in slabs:
                copy(wr.at[h, p], wr.at[h, p], wr_send.at[h, p], wr_recv.at[h, p], sibling).wait_recv()
                relay_copy(k, p).start()

    plane_slices()
    first(0)
    kp[...] = jnp.zeros_like(kp)
    screen(0)
    z_first()
    z_own(2)
    z_own(3)
    forward_y(0)
    first(1)
    screen(1)
    z_step(2, 0)
    z_step(3, 0)
    forward_x(0)
    forward_y(1)
    screen(2)
    z_step(2, 1)
    whole(0)
    half(0)
    forward_x(1)
    z_step(3, 1)
    z_step(2, 2)
    whole(1)
    half(1)
    z_step(3, 2)
    z_step(2, 3)
    whole(2)
    half(2)
    z_step(3, 3)
    relay(0)
    relay(1)
    whole(3)
    half(3)

    def operand(slot, core, p, value):
        rows = pl.ds(pl.multiple_of(core * ROWS, ROWS), ROWS)
        high, low = split(value)
        for where, part in ((0, high), (1, low), (2, high)):
            left[slot, rows, pl.ds((where * SLABS + p) * LANES, LANES)] = part
        if slot in (0, 2):
            for where, part in ((0, high), (1, high), (2, low)):
                right[slot // 2, rows, pl.ds((where * SLABS + p) * LANES, LANES)] = part

    def product(kind, core):
        rows, columns = ((0, 0), (1, 1), (1, 0), (2, 0), (3, 0), (3, 1))[kind]
        at = pl.ds(pl.multiple_of(core * ROWS, ROWS), ROWS)
        value = lax.dot_general(
            left[rows], right[columns, at], (((1,), (1,)), ((), ())), preferred_element_type=F32
        )
        rest = value[:, LANES:ROWS].reshape(8, 2, STRIP // 2, ROWS - LANES)
        rest = jnp.concatenate([rest[:, 0], rest[:, 1]], axis=-1)
        kp[core, kind, :, 0:STRIP] += value[:, 0:LANES].reshape(8, STRIP, LANES)
        kp[core, kind, :, STRIP:PACK] += rest

    def kinds_of(g):
        start, count = ((0, 1), (1, 1), (2, 2), (4, 1), (5, 1))[g]
        return pl.ds(start, count)

    def core_copy(g):
        kinds = kinds_of(g)
        return copy(kp.at[sib, kinds], rc.at[kinds], core_send.at[g], core_recv.at[g], sibling)

    def core_arrival(g):
        kinds = kinds_of(g)
        return copy(rc.at[kinds], rc.at[kinds], core_send.at[g], core_recv.at[g], sibling)

    def take_o(q):
        copy(ho.at[q], ho.at[q], h_send.at[2 * q + c, 2], ho_recv.at[q], sibling).wait_recv()
        for p in range(SLABS):
            operand(0, c, p, hs[2 * q + c, p])
            operand(0, sib, p, ho[q, p])

    def take_y_x(q):
        k = 2 * q + c
        for core in range(2):
            copy(hy.at[q, core], hy.at[q, core], h_send.at[k, 0], hy_recv.at[q, core], sibling).wait_recv()
            copy(hx.at[q, core], hx.at[q, core], h_send.at[k, 1], hx_recv.at[q, core], sibling).wait_recv()
        for p in range(SLABS):
            for core in range(2):
                operand(1, core, p, hy[q, core, p])
                operand(2, core, p, hx[q, core, p])

    def products_y_x(q):
        for core in (sib, c):
            product(1, core)
            if q == 1 and core is sib:
                core_copy(1).start()
            product(2, core)
            pl.when(xl == q)(functools.partial(product, 3, core))
            if q == 1 and core is sib:
                core_copy(2).start()

    def products_w(q):
        @pl.when(w_half(y, c) == q)
        def _():
            for p in range(SLABS):
                for core in range(2):
                    piece = hw.at[core, p]
                    copy(piece, piece, wr_send.at[core, p], hw_recv.at[core, p], sibling).wait_recv()
                    operand(3, core, p, hw[core, p])
            product(4, sib)
            if q == 1:
                core_copy(3).start()
            product(5, sib)
            if q == 1:
                core_copy(4).start()
            product(4, c)
            product(5, c)

        if q == 1:

            @pl.when(w_half(y, c) != q)
            def _():
                core_copy(3).start()
                core_copy(4).start()

    mine = jnp.where(xh == y // 2, 0, 1)

    def far_slice(s):
        return (z + 8 + far * (4 - s)) % 8

    def near_slice(s):
        return (z + 8 - far * (3 - s)) % 8

    def far_copy(s, g):
        src = rc.at[kinds_of(g), far_slice(s)]
        return copy(src, rp.at[s, kinds_of(g)], p_send.at[s, g], p_recv.at[s, g], z_far)

    def near_copy(s, g):
        src = rc.at[kinds_of(g), near_slice(s)]
        return copy(src, rm.at[s, kinds_of(g)], m_send.at[s, g], m_recv.at[s, g], z_near)

    def last_copy(which, kind):
        same = mine == kind % 2
        at = 4 if which == 2 else jnp.where(same, which, which + 2)
        piece = (z, far_slice(3), near_slice(2))[(which + 1) % 3]
        to = jnp.where(same, xh, 1 - xh) * 8 + piece
        return copy(rc.at[kind, piece], fin.at[at, kind], l_send.at[which, kind], l_recv.at[at, kind], (to, r))

    def sum_step(s, g):
        kinds = kinds_of(g)
        each_kind = range(kinds.start, kinds.start + kinds.size)
        if s == 0:
            core_arrival(g).wait_recv()

            def add(d, _):
                rc[kinds, d] = rc[kinds, d] + kp[c, kinds, d]
                return 0

            lax.fori_loop(0, 8, add, 0)
        else:
            far_copy(s - 1, g).wait_recv()
            d = far_slice(s)
            rc[kinds, d] = rc[kinds, d] + rp[s - 1, kinds]
            if s < 3:
                near_copy(s - 1, g).wait_recv()
                d = near_slice(s)
                rc[kinds, d] = rc[kinds, d] + rm[s - 1, kinds]
        if s < 3:
            far_copy(s, g).start()
        else:
            for kind in each_kind:
                last_copy(0, kind).start()
        if s < 2:
            near_copy(s, g).start()
        elif s == 2:
            for kind in each_kind:
                last_copy(1, kind).start()
        if s == 0:
            for kind in each_kind:
                pl.when(mine != kind % 2)(last_copy(2, kind).start)

    def strip_copies(n):
        i_y = y + (mine, 1 - mine, 2)[n]
        i_x = (xl + mine) % 2 if n == 1 else xl
        j_x = xl if n == 1 else (xl + mine) % 2
        at_i = row_of(i_y, i_x, z // 4)
        at_j = row_of(y, j_x, c)
        straight = ((at_i, at_j), rd.at[z % 4], f_recv.at[0])
        turned = ((at_j, at_i), rt.at[z % 4], f_recv.at[1])
        return fp.at[n], straight, turned

    def each_strip(n, local, remote):
        src, *targets = strip_copies(n)
        for which, (to, dst, recv) in enumerate(targets):
            own = jnp.logical_and(to[0] == a, to[1] == r)
            wanted = jnp.logical_or(mine == 1, which == 0) if n == 0 else True

            if local is not None:

                @pl.when(jnp.logical_and(wanted, own))
                def _(dst=dst, recv=recv):
                    local(pltpu.make_async_copy(src, dst, recv))

            @pl.when(jnp.logical_and(wanted, jnp.logical_not(own)))
            def _(dst=dst, recv=recv, to=to, which=which):
                remote(copy(src, dst, f_send.at[n, which], recv, to))

    def hand_out(n):
        kind = 2 * n + mine
        for at in range(5):
            piece = fin.at[at, kind]
            copy(piece, piece, l_send.at[0, kind], l_recv.at[at, kind], sibling).wait_recv()
        fp[n] = (rc[kind, z] + fin[0, kind] + fin[1, kind]) + (fin[2, kind] + fin[3, kind] + fin[4, kind])
        each_strip(n, lambda one: one.start(), lambda one: one.start())

    def handed_out(n):
        each_strip(n, None, lambda one: one.wait_send())

    take_o(0)
    product(0, sib)
    product(0, c)
    take_y_x(0)
    relay(2)
    products_y_x(0)
    relay(3, (0,))
    products_w(0)
    relay(3, (1, 2))
    take_o(1)
    product(0, sib)
    core_copy(0).start()
    product(0, c)
    take_y_x(1)
    products_y_x(1)
    sum_step(0, 0)
    sum_step(0, 1)
    sum_step(1, 0)
    sum_step(0, 2)
    products_w(1)
    sum_step(1, 1)
    sum_step(0, 3)
    sum_step(0, 4)
    sum_step(2, 0)
    sum_step(1, 2)
    sum_step(2, 1)
    sum_step(1, 3)
    sum_step(1, 4)
    sum_step(3, 0)
    sum_step(2, 2)
    sum_step(3, 1)
    sum_step(2, 3)
    sum_step(2, 4)
    sum_step(3, 2)
    sum_step(3, 3)
    sum_step(3, 4)
    hand_out(0)
    hand_out(1)
    hand_out(2)

    def sent(k, _):
        to_1, to_2, to_3 = h_copies(k)
        to_1.wait_send()
        to_2.wait_send()
        pl.when(k % 2 != c)(to_3.wait_send)
        for p in range(SLABS):
            pl.when(sends_w(k))(w_copy(k, p).wait_send)
            pl.when(relays(k))(relay_copy(k, p).wait_send)
        return 0

    def sent_plane(k, _):
        for j in range(3):
            to_y(k, j).wait_send()
        for j in range(4):
            for part in range(2):
                to_x(k, j, here, part).wait_send()
        for j in range(8):
            to_sibling(k, j, here, c).wait_send()
        return 0

    def sent_z(k, _):
        for s in range(4):
            to_far(k, s).wait_send()
        for s in range(3):
            to_near(k, s).wait_send()
        for j in range(8):
            z_sibling(k, c, j).wait_send()
        return 0

    lax.fori_loop(0, CHUNKS, sent, 0)
    lax.fori_loop(0, PLANE, sent_plane, 0)
    lax.fori_loop(PLANE, CHUNKS, sent_z, 0)
    for j in range(7):
        slices(j, here).wait_send()
    for g in range(5):
        core_copy(g).wait_send()
        for s in range(3):
            far_copy(s, g).wait_send()
        for s in range(2):
            near_copy(s, g).wait_send()

    for kind in range(6):
        for which in range(2):
            last_copy(which, kind).wait_send()
        pl.when(mine != kind % 2)(last_copy(2, kind).wait_send)

    apart = (y - a // 4 + 4) % 4
    across_x = xl != (a // 2) % 2

    def gather(strips, sem, block):
        pltpu.make_async_copy(strips, strips, sem).wait()
        for n in range(4):
            rest = strips[n, STRIP:PACK]
            at = n * STRIP
            block[at : at + STRIP, 0:LANES] = strips[n, 0:STRIP]
            block[at : at + STRIP // 2, LANES:ROWS] = rest[:, 0 : ROWS - LANES]
            block[at + STRIP // 2 : at + STRIP, LANES:ROWS] = rest[:, ROWS - LANES : LANES]

    @pl.when(apart != 1)
    def _():
        gather(rd, f_recv.at[0], out)

    @pl.when(apart == 1)
    def _():
        out[...] = jnp.zeros_like(out)

    @pl.when(jnp.logical_and(apart != 3, jnp.logical_or(apart != 0, across_x)))
    def _():
        gather(rt, f_recv.at[1], ft)
        out[...] = out[...] + ft[...].T

    for n in range(3):
        handed_out(n)


def per_device(factors, orbitals, tile_mask):
    dma = pltpu.SemaphoreType.DMA
    vmem = pltpu.VMEM
    part = (SLABS, ROWS, LANES)
    return pl.pallas_call(
        kernel,
        out_shape=jax.ShapeDtypeStruct((ROWS, ROWS), F32),
        in_specs=[
            pl.BlockSpec(memory_space=pl.ANY),
            pl.BlockSpec(memory_space=pltpu.VMEM),
            pl.BlockSpec(memory_space=pltpu.SMEM),
        ],
        out_specs=pl.BlockSpec(memory_space=pltpu.VMEM),
        scratch_shapes=[
            vmem((SLABS, ROWS, 3072), F32),
            vmem((SLABS, ROWS, 3072), BF16),
            vmem((SLABS, ROWS, 3072), BF16),
            vmem((CHUNKS, 2, 8, ROWS, LANES), F32),
            vmem((3072, 2 * LANES), BF16),
            vmem((CHUNKS, *part), F32),
            vmem((2, *part), F32),
            vmem((2, 2, *part), F32),
            vmem((2, 2, *part), F32),
            vmem((2, *part), F32),
            vmem((2, *part), F32),
            vmem((4, PAIR, 3 * SLABS * LANES), BF16),
            vmem((2, PAIR, 3 * SLABS * LANES), BF16),
            vmem((2, 6, 8, PACK, LANES), F32),
            vmem((6, 8, PACK, LANES), F32),
            vmem((3, 6, PACK, LANES), F32),
            vmem((2, 6, PACK, LANES), F32),
            vmem((5, 6, PACK, LANES), F32),
            vmem((3, PACK, LANES), F32),
            vmem((4, PACK, LANES), F32),
            vmem((4, PACK, LANES), F32),
            vmem((ROWS, ROWS), F32),
            dma((SLABS,)),
            dma((CHUNKS, 3)), dma((CHUNKS, 3)),
            dma((CHUNKS, 4, 2)), dma((CHUNKS, 4, 2)),
            dma((CHUNKS, 8)), dma((CHUNKS, 8)),
            dma((7,)), dma((7,)), dma((CHUNKS, 4)), dma((CHUNKS, 4)), dma((CHUNKS, 3)), dma((CHUNKS, 3)),
            dma((CHUNKS, 8)), dma((CHUNKS, 8)),
            dma((CHUNKS, 3)), dma((CHUNKS, SLABS)), dma((2,)), dma((2, 2)), dma((2, 2)),
            dma((2, SLABS)), dma((2, SLABS)), dma((2, SLABS)),
            dma((5,)), dma((5,)),
            dma((3, 5)), dma((3, 5)), dma((2, 5)), dma((2, 5)),
            dma((3, 6)), dma((5, 6)),
            dma((3, 2)), dma((2,)),
        ],
        compiler_params=pltpu.CompilerParams(
            collective_id=0, has_side_effects=True, vmem_limit_bytes=60 * 2**20
        ),
    )(factors, orbitals, tile_mask)


def solution(mesh):
    placed = (P("aux", "row", None), P("row", None), P("aux", None, None))
    return jax.shard_map(
        per_device, mesh=mesh, in_specs=placed, out_specs=P("aux", "row"), check_vma=False
    )
```

```python
import functools

import jax
import jax.numpy as jnp
from jax import lax
from jax.experimental import pallas as pl
from jax.experimental.pallas import tpu as pltpu
from jax.sharding import PartitionSpec as P

F32 = jnp.float32
BF16 = jnp.bfloat16
MESH = pl.DeviceIdType.MESH
ROWS = 192
PAIR = 384
LANES = 128
CHUNKS = 4
PLANE = 2
SLICE = 24
SLABS = 3
STRIP = 48
PACK = 72
STEPS_Y = (1, -1, 2)


def split(value):
    high = value.astype(BF16)
    return high, (value - high.astype(F32)).astype(BF16)


def kernel(
    b_hbm, c_ref, mask, out,
    bf, bh, bl, cb, ch, hs, ho, hy, hx, hw, wr, left, right, kp, rc, rp, rm, fin, fp, rd, rt, ft,
    sem_b, y_send, y_recv, x_send, x_recv, s_send, s_recv,
    g_send, g_recv, long_send, long_recv, short_send, short_recv, zs_send, zs_recv,
    h_send, w_send, ho_recv, hy_recv, hx_recv, hw_recv, wr_send, wr_recv,
    core_send, core_recv, p_send, p_recv, m_send, m_recv, l_send, l_recv, f_send, f_recv,
):
    a, r = lax.axis_index("aux"), lax.axis_index("row")
    xh, z = a // 8, a % 8
    y, xl, c = r // 4, (r // 2) % 2, r % 2
    sib = 1 - c

    def row_of(yy, xx, cc):
        return ((yy + 4) % 4 * 2 + xx) * 2 + cc

    def dev(yy, xx, cc):
        return (a, row_of(yy, xx, cc))

    def copy(src, dst, send, recv, to):
        return pltpu.make_async_remote_copy(
            src_ref=src, dst_ref=dst, send_sem=send, recv_sem=recv, device_id=to, device_id_type=MESH
        )

    across = ((a, row_of(y, 1 - xl, c)), ((1 - xh) * 8 + z, row_of(y, 1 - xl, c)))
    sibling = dev(y, xl, sib)
    z_up = (xh * 8 + (z + 1) % 8, r)
    z_down = (xh * 8 + (z + 7) % 8, r)

    slab_copies = [pltpu.make_async_copy(b_hbm.at[p], bf.at[p], sem_b.at[p]) for p in range(SLABS)]
    for each in slab_copies:
        each.start()

    here = 2 * y + xl
    for k in range(CHUNKS):
        cb[k, c, here] = c_ref[:, k * LANES : (k + 1) * LANES]

    barrier = pltpu.get_barrier_semaphore()
    peers = [dev(y + dy, xl, c) for dy in STEPS_Y] + [dev(y + dy, 1 - xl, c) for dy in (0, *STEPS_Y)]
    greeted = [
        *peers, across[1], sibling, z_up, z_down,
    ]
    for each in greeted:
        pl.semaphore_signal(barrier, inc=1, device_id=each, device_id_type=MESH)
    pl.semaphore_wait(barrier, len(greeted))

    def place(yy, xx):
        return (yy + 4) % 4 * 2 + xx

    def to_y(k, j):
        block = cb.at[k, c, here]
        return copy(block, block, y_send.at[k, j], y_recv.at[k, j], dev(y + STEPS_Y[j], xl, c))

    def from_y(k, j):
        block = cb.at[k, c, place(y - STEPS_Y[j], xl)]
        return copy(block, block, y_send.at[k, j], y_recv.at[k, j], sibling)

    def to_x(k, j, at, part):
        piece = cb.at[k, c, at, pl.ds(96 * part, 96)]
        return copy(piece, piece, x_send.at[k, j, part], x_recv.at[k, j, part], across[part])

    def to_sibling(k, j, at, core):
        block = cb.at[k, core, at]
        return copy(block, block, s_send.at[k, j], s_recv.at[k, j], sibling)

    def y_place(j, xx):
        return place(y - STEPS_Y[j], xx) if j < 3 else place(y, xx)

    def first(k):
        for j in range(3):
            to_y(k, j).start()
        for part in range(2):
            to_x(k, 3, here, part).start()
        to_sibling(k, 3, here, c).start()

    def forward_y(k):
        for j in range(3):
            from_y(k, j).wait_recv()
            at = y_place(j, xl)
            for part in range(2):
                to_x(k, j, at, part).start()
            to_sibling(k, j, at, c).start()

    def forward_x(k):
        for j in (3, 0, 1, 2):
            at = y_place(j, 1 - xl)
            for part in range(2):
                to_x(k, j, at, part).wait_recv()
            to_sibling(k, 4 + j, at, c).start()

    def slices(j, at):
        piece = cb.at[pl.ds(PLANE, CHUNKS - PLANE), c, at, pl.ds(SLICE * z, SLICE)]
        return copy(piece, piece, g_send.at[j], g_recv.at[j], peers[j])

    far = 1 - 2 * c
    z_far = (xh * 8 + (z + 8 + far) % 8, r)
    z_near = (xh * 8 + (z + 8 - far) % 8, r)

    def z_piece(k, core, at):
        return cb.at[k, core, :, pl.ds(SLICE * ((z + 8 + at) % 8), SLICE)]

    def to_far(k, s):
        piece = z_piece(k, c, -far * s)
        return copy(piece, piece, long_send.at[k, s], long_recv.at[k, s], z_far)

    def from_far(k, s):
        piece = z_piece(k, c, -far * (s + 1))
        return copy(piece, piece, long_send.at[k, s], long_recv.at[k, s], z_far)

    def to_near(k, s):
        piece = z_piece(k, c, far * s)
        return copy(piece, piece, short_send.at[k, s], short_recv.at[k, s], z_near)

    def from_near(k, s):
        piece = z_piece(k, c, far * (s + 1))
        return copy(piece, piece, short_send.at[k, s], short_recv.at[k, s], z_near)

    def z_sibling(k, core, j):
        piece = z_piece(k, core, j)
        at = (j + 8) % 8
        return copy(piece, piece, zs_send.at[k, at], zs_recv.at[k, at], sibling)

    def plane_slices():
        for j in range(7):
            slices(j, here).start()

    def z_first():
        for j in range(7):
            at = place(y - STEPS_Y[j], xl) if j < 3 else place(y, 1 - xl) if j == 3 else place(y - STEPS_Y[j - 4], 1 - xl)
            slices(j, at).wait_recv()

    def z_own(k):
        to_far(k, 0).start()
        to_near(k, 0).start()
        z_sibling(k, c, 0).start()

    def z_step(k, s):
        from_far(k, s).wait_recv()
        if s < 3:
            to_far(k, s + 1).start()
        z_sibling(k, c, -far * (s + 1)).start()
        if s < 3:
            from_near(k, s).wait_recv()
            if s < 2:
                to_near(k, s + 1).start()
            z_sibling(k, c, far * (s + 1)).start()

    def whole(k):
        if k < PLANE:
            for j in range(4):
                to_sibling(k, j, y_place(j, xl), sib).wait_recv()
                to_sibling(k, 4 + j, y_place(j, 1 - xl), sib).wait_recv()
        else:
            for j in range(8):
                z_sibling(k, sib, j).wait_recv()

    def screen(p):
        slab_copies[p].wait()

        def tile(n, _):
            at = pl.ds(pl.multiple_of(n * LANES, LANES), LANES)
            for g in range(3):
                keep = mask[p, (3 * r + g) // 2, n].astype(F32)
                rows = pl.ds(64 * g, 64)
                high, low = split(bf[p, rows, at] * keep)
                bh[p, rows, at] = high
                bl[p, rows, at] = low
            return 0

        lax.fori_loop(0, 24, tile, 0, unroll=4)

    def half(k):
        def block(n, _):
            high, low = split(cb[k, n % 2, n // 2])
            at = pl.ds(pl.multiple_of(n * ROWS, ROWS), ROWS)
            ch[at, 0:LANES] = high
            ch[at, LANES : 2 * LANES] = low
            return 0

        lax.fori_loop(0, 16, block, 0)

        for p in range(SLABS):
            both = jnp.dot(bh[p], ch[...], preferred_element_type=F32)
            low = jnp.dot(bl[p], ch[:, 0:LANES], preferred_element_type=F32)
            hs[k, p] = both[:, 0:LANES] + (both[:, LANES : 2 * LANES] + low)
            send_half(k, p)

    def h_copies(k, p=slice(None)):
        h, q = k % 2, k // 2
        src = hs.at[k, p]
        return (
            copy(src, hy.at[q, c, p], h_send.at[k, 0], hy_recv.at[q, c], dev(y - 1, xl, h)),
            copy(src, hx.at[q, c, p], h_send.at[k, 1], hx_recv.at[q, c], dev(y, 1 - xl, h)),
            copy(src, ho.at[q, p], h_send.at[k, 2], ho_recv.at[q], sibling),
        )

    def w_copy(k, p):
        h = k % 2
        return copy(hs.at[k, p], wr.at[h, p], w_send.at[k, p], wr_recv.at[h, p], dev(y + 1, xl, c))

    def w_half(yy, core):
        return ((yy + 4) % 4 // 2 + core) % 2

    def sends_w(k):
        return k // 2 == w_half(y + 2, k % 2)

    def send_half(k, p):
        pl.when(sends_w(k))(w_copy(k, p).start)
        to_1, to_2, to_3 = h_copies(k, p)
        to_1.start()
        to_2.start()
        pl.when(k % 2 != c)(to_3.start)

    def relay_copy(k, p):
        h = k % 2
        return copy(wr.at[h, p], hw.at[c, p], wr_send.at[h, p], hw_recv.at[c, p], dev(y + 1, xl, h))

    def relays(k):
        return k // 2 == w_half(y + 1, k % 2)

    def relay(k, slabs=range(SLABS)):
        @pl.when(relays(k))
        def _():
            h = k % 2
            for p in slabs:
                copy(wr.at[h, p], wr.at[h, p], wr_send.at[h, p], wr_recv.at[h, p], sibling).wait_recv()
                relay_copy(k, p).start()

    plane_slices()
    first(0)
    kp[...] = jnp.zeros_like(kp)
    screen(0)
    z_first()
    z_own(2)
    z_own(3)
    forward_y(0)
    first(1)
    screen(1)
    z_step(2, 0)
    z_step(3, 0)
    forward_x(0)
    forward_y(1)
    screen(2)
    z_step(2, 1)
    whole(0)
    half(0)
    forward_x(1)
    z_step(3, 1)
    z_step(2, 2)
    whole(1)
    half(1)
    z_step(3, 2)
    z_step(2, 3)
    whole(2)
    half(2)
    z_step(3, 3)
    relay(0)
    relay(1)
    whole(3)
    half(3)

    def operand(slot, core, p, value):
        rows = pl.ds(pl.multiple_of(core * ROWS, ROWS), ROWS)
        high, low = split(value)
        for where, part in ((0, high), (1, low), (2, high)):
            left[slot, rows, pl.ds((where * SLABS + p) * LANES, LANES)] = part
        if slot in (0, 2):
            for where, part in ((0, high), (1, high), (2, low)):
                right[slot // 2, rows, pl.ds((where * SLABS + p) * LANES, LANES)] = part

    def product(kind, core):
        rows, columns = ((0, 0), (1, 1), (1, 0), (2, 0), (3, 0), (3, 1))[kind]
        at = pl.ds(pl.multiple_of(core * ROWS, ROWS), ROWS)
        value = lax.dot_general(
            left[rows], right[columns, at], (((1,), (1,)), ((), ())), preferred_element_type=F32
        )
        rest = value[:, LANES:ROWS].reshape(8, 2, STRIP // 2, ROWS - LANES)
        rest = jnp.concatenate([rest[:, 0], rest[:, 1]], axis=-1)
        body = value[:, 0:LANES].reshape(8, STRIP, LANES)
        base = 4 * ((y + (0, 1, 0, 2)[rows]) % 2) + 2 * ((xl + (rows == 2)) % 2)
        for n in range(8):
            at_z = (base + 8 + (-n if n < 4 else n - 3)) % 8
            kp[core, kind, at_z, 0:STRIP] += body[n]
            kp[core, kind, at_z, STRIP:PACK] += rest[n]

    def kinds_of(g):
        start, count = ((0, 1), (1, 1), (2, 2), (4, 1), (5, 1))[g]
        return pl.ds(start, count)

    def core_copy(g):
        kinds = kinds_of(g)
        return copy(kp.at[sib, kinds], rc.at[kinds], core_send.at[g], core_recv.at[g], sibling)

    def core_arrival(g):
        kinds = kinds_of(g)
        return copy(rc.at[kinds], rc.at[kinds], core_send.at[g], core_recv.at[g], sibling)

    def take_o(q):
        copy(ho.at[q], ho.at[q], h_send.at[2 * q + c, 2], ho_recv.at[q], sibling).wait_recv()
        for p in range(SLABS):
            operand(0, c, p, hs[2 * q + c, p])
            operand(0, sib, p, ho[q, p])

    def take_y_x(q):
        k = 2 * q + c
        for core in range(2):
            copy(hy.at[q, core], hy.at[q, core], h_send.at[k, 0], hy_recv.at[q, core], sibling).wait_recv()
            copy(hx.at[q, core], hx.at[q, core], h_send.at[k, 1], hx_recv.at[q, core], sibling).wait_recv()
        for p in range(SLABS):
            for core in range(2):
                operand(1, core, p, hy[q, core, p])
                operand(2, core, p, hx[q, core, p])

    def products_y_x(q):
        for core in (sib, c):
            product(1, core)
            if q == 1 and core is sib:
                core_copy(1).start()
            product(2, core)
            pl.when(xl == q)(functools.partial(product, 3, core))
            if q == 1 and core is sib:
                core_copy(2).start()

    def products_w(q):
        @pl.when(w_half(y, c) == q)
        def _():
            for p in range(SLABS):
                for core in range(2):
                    piece = hw.at[core, p]
                    copy(piece, piece, wr_send.at[core, p], hw_recv.at[core, p], sibling).wait_recv()
                    operand(3, core, p, hw[core, p])
            product(4, sib)
            if q == 1:
                core_copy(3).start()
            product(5, sib)
            if q == 1:
                core_copy(4).start()
            product(4, c)
            product(5, c)

        if q == 1:

            @pl.when(w_half(y, c) != q)
            def _():
                core_copy(3).start()
                core_copy(4).start()

    mine = jnp.where(xh == y // 2, 0, 1)

    def far_slice(s):
        return (z + 8 + far * (4 - s)) % 8

    def near_slice(s):
        return (z + 8 - far * (3 - s)) % 8

    def far_copy(s, g):
        src = rc.at[kinds_of(g), far_slice(s)]
        return copy(src, rp.at[s, kinds_of(g)], p_send.at[s, g], p_recv.at[s, g], z_far)

    def near_copy(s, g):
        src = rc.at[kinds_of(g), near_slice(s)]
        return copy(src, rm.at[s, kinds_of(g)], m_send.at[s, g], m_recv.at[s, g], z_near)

    def last_copy(which, kind):
        same = mine == kind % 2
        at = 4 if which == 2 else jnp.where(same, which, which + 2)
        piece = (z, far_slice(3), near_slice(2))[(which + 1) % 3]
        to = jnp.where(same, xh, 1 - xh) * 8 + piece
        return copy(rc.at[kind, piece], fin.at[at, kind], l_send.at[which, kind], l_recv.at[at, kind], (to, r))

    def sum_step(s, g):
        kinds = kinds_of(g)
        each_kind = range(kinds.start, kinds.start + kinds.size)
        if s == 0:
            core_arrival(g).wait_recv()

            def add(d, _):
                rc[kinds, d] = rc[kinds, d] + kp[c, kinds, d]
                return 0

            lax.fori_loop(0, 8, add, 0)
        else:
            far_copy(s - 1, g).wait_recv()
            d = far_slice(s)
            rc[kinds, d] = rc[kinds, d] + rp[s - 1, kinds]
            if s < 3:
                near_copy(s - 1, g).wait_recv()
                d = near_slice(s)
                rc[kinds, d] = rc[kinds, d] + rm[s - 1, kinds]
        if s < 3:
            far_copy(s, g).start()
        else:
            for kind in each_kind:
                last_copy(0, kind).start()
        if s < 2:
            near_copy(s, g).start()
        elif s == 2:
            for kind in each_kind:
                last_copy(1, kind).start()
        if s == 0:
            for kind in each_kind:
                pl.when(mine != kind % 2)(last_copy(2, kind).start)

    def strip_copies(n):
        i_y = y + (mine, 1 - mine, 2)[n]
        i_x = (xl + mine) % 2 if n == 1 else xl
        j_x = xl if n == 1 else (xl + mine) % 2
        above = (z + 8 - (4 * (i_y % 2) + 2 * i_x)) % 8
        upper = jnp.logical_and(above >= 1, above <= 4)
        strip = jnp.where(upper, above - 1, (8 - above) % 8)
        at_i = row_of(i_y, i_x, jnp.where(upper, 1, 0))
        at_j = row_of(y, j_x, c)
        straight = ((at_i, at_j), rd.at[strip], f_recv.at[0])
        turned = ((at_j, at_i), rt.at[strip], f_recv.at[1])
        return fp.at[n], straight, turned

    def each_strip(n, local, remote):
        src, *targets = strip_copies(n)
        for which, (to, dst, recv) in enumerate(targets):
            own = jnp.logical_and(to[0] == a, to[1] == r)
            wanted = jnp.logical_or(mine == 1, which == 0) if n == 0 else True

            if local is not None:

                @pl.when(jnp.logical_and(wanted, own))
                def _(dst=dst, recv=recv):
                    local(pltpu.make_async_copy(src, dst, recv))

            @pl.when(jnp.logical_and(wanted, jnp.logical_not(own)))
            def _(dst=dst, recv=recv, to=to, which=which):
                remote(copy(src, dst, f_send.at[n, which], recv, to))

    def hand_out(n):
        kind = 2 * n + mine
        for at in range(5):
            piece = fin.at[at, kind]
            copy(piece, piece, l_send.at[0, kind], l_recv.at[at, kind], sibling).wait_recv()
        fp[n] = (rc[kind, z] + fin[0, kind] + fin[1, kind]) + (fin[2, kind] + fin[3, kind] + fin[4, kind])
        each_strip(n, lambda one: one.start(), lambda one: one.start())

    def handed_out(n):
        each_strip(n, None, lambda one: one.wait_send())

    take_o(0)
    product(0, sib)
    product(0, c)
    take_y_x(0)
    relay(2)
    products_y_x(0)
    relay(3, (0,))
    products_w(0)
    relay(3, (1, 2))
    take_o(1)
    product(0, sib)
    core_copy(0).start()
    product(0, c)
    take_y_x(1)
    products_y_x(1)
    sum_step(0, 0)
    sum_step(0, 1)
    sum_step(0, 2)
    sum_step(1, 0)
    products_w(1)
    sum_step(1, 1)
    sum_step(0, 3)
    sum_step(0, 4)
    sum_step(1, 2)
    sum_step(2, 0)
    sum_step(2, 1)
    sum_step(1, 3)
    sum_step(1, 4)
    sum_step(3, 0)
    sum_step(3, 1)
    sum_step(2, 2)
    sum_step(2, 3)
    sum_step(2, 4)
    sum_step(3, 2)
    hand_out(0)
    sum_step(3, 3)
    sum_step(3, 4)
    hand_out(1)
    hand_out(2)

    def sent(k, _):
        to_1, to_2, to_3 = h_copies(k)
        to_1.wait_send()
        to_2.wait_send()
        pl.when(k % 2 != c)(to_3.wait_send)
        for p in range(SLABS):
            pl.when(sends_w(k))(w_copy(k, p).wait_send)
            pl.when(relays(k))(relay_copy(k, p).wait_send)
        return 0

    def sent_plane(k, _):
        for j in range(3):
            to_y(k, j).wait_send()
        for j in range(4):
            for part in range(2):
                to_x(k, j, here, part).wait_send()
        for j in range(8):
            to_sibling(k, j, here, c).wait_send()
        return 0

    def sent_z(k, _):
        for s in range(4):
            to_far(k, s).wait_send()
        for s in range(3):
            to_near(k, s).wait_send()
        for j in range(8):
            z_sibling(k, c, j).wait_send()
        return 0

    lax.fori_loop(0, CHUNKS, sent, 0)
    lax.fori_loop(0, PLANE, sent_plane, 0)
    lax.fori_loop(PLANE, CHUNKS, sent_z, 0)
    for j in range(7):
        slices(j, here).wait_send()
    for g in range(5):
        core_copy(g).wait_send()
        for s in range(3):
            far_copy(s, g).wait_send()
        for s in range(2):
            near_copy(s, g).wait_send()

    for kind in range(6):
        for which in range(2):
            last_copy(which, kind).wait_send()
        pl.when(mine != kind % 2)(last_copy(2, kind).wait_send)

    apart = (y - a // 4 + 4) % 4
    across_x = xl != (a // 2) % 2

    def gather(strips, sem, block):
        pltpu.make_async_copy(strips, strips, sem).wait()
        for n in range(4):
            rest = strips[n, STRIP:PACK]
            at = n * STRIP
            block[at : at + STRIP, 0:LANES] = strips[n, 0:STRIP]
            block[at : at + STRIP // 2, LANES:ROWS] = rest[:, 0 : ROWS - LANES]
            block[at + STRIP // 2 : at + STRIP, LANES:ROWS] = rest[:, ROWS - LANES : LANES]

    @pl.when(apart != 1)
    def _():
        gather(rd, f_recv.at[0], out)

    @pl.when(apart == 1)
    def _():
        out[...] = jnp.zeros_like(out)

    @pl.when(jnp.logical_and(apart != 3, jnp.logical_or(apart != 0, across_x)))
    def _():
        gather(rt, f_recv.at[1], ft)
        out[...] = out[...] + ft[...].T

    for n in range(3):
        handed_out(n)


def per_device(factors, orbitals, tile_mask):
    dma = pltpu.SemaphoreType.DMA
    vmem = pltpu.VMEM
    part = (SLABS, ROWS, LANES)
    return pl.pallas_call(
        kernel,
        out_shape=jax.ShapeDtypeStruct((ROWS, ROWS), F32),
        in_specs=[
            pl.BlockSpec(memory_space=pl.ANY),
            pl.BlockSpec(memory_space=pltpu.VMEM),
            pl.BlockSpec(memory_space=pltpu.SMEM),
        ],
        out_specs=pl.BlockSpec(memory_space=pltpu.VMEM),
        scratch_shapes=[
            vmem((SLABS, ROWS, 3072), F32),
            vmem((SLABS, ROWS, 3072), BF16),
            vmem((SLABS, ROWS, 3072), BF16),
            vmem((CHUNKS, 2, 8, ROWS, LANES), F32),
            vmem((3072, 2 * LANES), BF16),
            vmem((CHUNKS, *part), F32),
            vmem((2, *part), F32),
            vmem((2, 2, *part), F32),
            vmem((2, 2, *part), F32),
            vmem((2, *part), F32),
            vmem((2, *part), F32),
            vmem((4, PAIR, 3 * SLABS * LANES), BF16),
            vmem((2, PAIR, 3 * SLABS * LANES), BF16),
            vmem((2, 6, 8, PACK, LANES), F32),
            vmem((6, 8, PACK, LANES), F32),
            vmem((3, 6, PACK, LANES), F32),
            vmem((2, 6, PACK, LANES), F32),
            vmem((5, 6, PACK, LANES), F32),
            vmem((3, PACK, LANES), F32),
            vmem((4, PACK, LANES), F32),
            vmem((4, PACK, LANES), F32),
            vmem((ROWS, ROWS), F32),
            dma((SLABS,)),
            dma((CHUNKS, 3)), dma((CHUNKS, 3)),
            dma((CHUNKS, 4, 2)), dma((CHUNKS, 4, 2)),
            dma((CHUNKS, 8)), dma((CHUNKS, 8)),
            dma((7,)), dma((7,)), dma((CHUNKS, 4)), dma((CHUNKS, 4)), dma((CHUNKS, 3)), dma((CHUNKS, 3)),
            dma((CHUNKS, 8)), dma((CHUNKS, 8)),
            dma((CHUNKS, 3)), dma((CHUNKS, SLABS)), dma((2,)), dma((2, 2)), dma((2, 2)),
            dma((2, SLABS)), dma((2, SLABS)), dma((2, SLABS)),
            dma((5,)), dma((5,)),
            dma((3, 5)), dma((3, 5)), dma((2, 5)), dma((2, 5)),
            dma((3, 6)), dma((5, 6)),
            dma((3, 2)), dma((2,)),
        ],
        compiler_params=pltpu.CompilerParams(
            collective_id=0, has_side_effects=True, vmem_limit_bytes=60 * 2**20
        ),
    )(factors, orbitals, tile_mask)


def solution(mesh):
    placed = (P("aux", "row", None), P("row", None), P("aux", None, None))
    return jax.shard_map(
        per_device, mesh=mesh, in_specs=placed, out_specs=P("aux", "row"), check_vma=False
    )
```
